512 devices in a mesh: gx: 32 (over y_lo, z), gy: 4 (over x), gz: 4 (over y_hi, core).
Axes of the slice: x: 4, y: 8 (y_hi: 2, y_lo: 4; y = y_hi * 4 + y_lo), z: 8, core: 2. Of those that a mesh axis runs over, the one named last changes fastest.
Arguments:
- initial_field: float32 [3, 256, 128, 512], P(None, 'gx', 'gy', 'gz'), may hold values from -6 to 6
- inv_permittivity: float32 [256, 128, 512], P('gx', 'gy', 'gz'), may hold values from 0.25 to 1
- history: bfloat16 [12288, 12, 256], P(('gx', 'gy', 'gz')), may hold values from -6 to 6
- tile_rows: int32 [12288], P(('gx', 'gy', 'gz')), may hold values from 0 to 255
- owners: int32 [12288, 1], P(('gx', 'gy', 'gz')), may hold values from 0 to 31; in each aligned block of 24 rows (0 to 23, 24 to 47, ...) at most 2 rows name the same one
- delays: int32 [12288, 4096], P(('gx', 'gy', 'gz')), may hold values from 0 to 3
- weights: bfloat16 [256, 4096], replicated, may hold values from -0.375 to 0.375
Outputs:
- efield: float32 [3, 256, 128, 512], P(None, 'gx', 'gy', 'gz')
- far_field: float32 [32, 20, 4096], P('gx', None, ('gy', 'gz'))
The draws below stay inside these ranges and needn't reach their ends.
Inputs may be any that keep to these rules, and one draw needn't show every extreme that they name: `owners`: among the 24 tiles of one device no section is named more than 2 times, a bound that some block reaches.
All inputs are finite; a program needn't handle non-finite values.
Results may differ from the reference program's by a relative error of at most 0.0014.
Values may be sent and summed in bfloat16 or wider, within the bound.
No kernel may reach another device: no remote copies, remote signals or barrier semaphores. Data moves between devices by JAX's collectives and lax.ppermute only.
A program may use at most 128 MiB of HBM per device.

```python
import math
import jax
import jax.numpy as jnp
import numpy as np
from jax import lax

CX = 8
CY = 32
CZ = 128
STEPS = 4
HIST = 16
LAG = 4
DIRS = 4096
FT = 24
CAP = 2
HPAST = 12
NB = 20
NX = 256
NY = 128
NZ = 512
TILES = 12288
N_GX = 32
N_GY = 4
N_GZ = 4


def touch_ends(drawn, key, low, largest):
    dims = drawn.shape
    spot = [jax.random.randint(jax.random.fold_in(key, axis), (), 0, dims[axis]) for axis in range(len(dims))]
    drawn = drawn.at[tuple(spot)].set(low)
    longest = dims.index(max(dims))
    spot[longest] = (spot[longest] + 1) % dims[longest]
    return drawn.at[tuple(spot)].set(largest)


def steps_of(stream_key, extent, shards, least, high):
    gain = 1.0
    for position, shards_of in shards:
        steps = jax.random.uniform(jax.random.fold_in(jax.random.fold_in(stream_key, 6), position), (shards_of,), jnp.float32, least / len(shards), high / len(shards))
        gain = gain * jnp.repeat(jnp.exp(steps), extent[position] // shards_of).reshape((-1,) + (1,) * (len(extent) - 1 - position))
    return gain


def shared_out(key, own, number, rows, amount, top, reach, skew):
    order = jax.random.permutation(key, amount)
    heavy_load, usual = load_shares(amount, rows * top, reach, skew, True), load_shares(amount, rows * top, reach, skew, False)
    places = jnp.arange(amount)

    def named(tallies, rotation):
        used = int((tallies > 0).sum())
        fixed = max(1, used // 4)
        moved = fixed + (places - fixed + rotation * (used - fixed)) % max(1, amount - fixed)
        return jnp.zeros((amount,), jnp.int32).at[order[jnp.where(places < fixed, places, moved)]].set(jnp.asarray(tallies, jnp.int32))

    tallies = jnp.where(number % 4 == 0, named(heavy_load, number // 4), named(usual, number - number // 4 - 1))
    mixed = jax.random.permutation(jax.random.fold_in(own, 3), amount)
    giver, sink = mixed[0:amount // 2 * 2:2], mixed[1:amount // 2 * 2:2]
    margin = jnp.minimum(tallies[giver] - 1, reach - tallies[sink]) // 2
    margin = jnp.where((giver == order[0]) | (sink == order[0]) | (tallies[sink] == 0), 0, jnp.maximum(margin, 0))
    moved = jax.random.randint(jax.random.fold_in(own, 4), (amount // 2,), 0, 1 << 20) % (margin + 1)
    tallies = tallies.at[giver].add(-moved).at[sink].add(moved)
    items = jnp.searchsorted(jnp.cumsum(tallies), jnp.arange(rows * top), side="right").astype(jnp.int32)
    grid = items.reshape(top, rows).T
    grid = grid[jax.random.permutation(jax.random.fold_in(own, 1), rows)]
    rotation = jax.random.randint(jax.random.fold_in(own, 2), (rows, 1), 0, top)
    return jnp.take_along_axis(grid, (jnp.arange(top)[None, :] + rotation) % top, axis=1)


def load_shares(amount, total, bound, lean, full):
    weights = [(1 << 20) // math.isqrt(standing ** lean) + 1 for standing in range(1, amount + 1)]
    largest = bound if full else min(bound, max(-(-total // amount), total * weights[0] // sum(weights)))
    least = 1 if total - largest >= amount - 1 else 0
    holding, spare = [largest] + [least] * (amount - 1), total - largest - least * (amount - 1)
    while spare > 0:
        movable = [i for i in range(1, amount) if holding[i] < largest] or [i for i in range(1, amount) if holding[i] < bound]
        whole, budget = sum([weights[i] for i in movable]), spare
        for i in movable:
            addition = min(bound - holding[i], max(1, budget * weights[i] // whole), spare)
            holding[i] = holding[i] + addition
            spare = spare - addition
    return np.array(holding)


def scatter_about(rng, shape, spread, limit, cuts=(), held_as=jnp.bfloat16):
    entries = jax.random.normal(rng, shape, jnp.float32) * spread
    if len(cuts) > 0:
        entries = steps_of(rng, shape, cuts, -0.22, 0.18) * entries
    return jnp.clip(entries, min=-limit, max=limit).astype(held_as)


def setup_inputs(seed: int = 0) -> dict:
    keys = jax.random.split(jax.random.key(seed), 8)
    initial_field = scatter_about(keys[0], (3, NX, NY, NZ), 1.0, 6.0, ((1, 32), (2, 4), (3, 4)), jnp.float32)
    inv_permittivity = jnp.clip(jnp.exp(math.log(1.0) - 1.3862944 * jax.random.uniform(keys[1], (NX, NY, NZ), jnp.float32) ** steps_of(keys[1], (NX, NY, NZ), ((0, 32), (1, 4), (2, 4)), -0.2, 0.2)), 0.25, 1.0)
    history = scatter_about(keys[2], (TILES, HPAST, 2 * CZ), 1.0, 6.0, ((0, 512),))
    tile_rows = touch_ends(jax.random.randint(keys[3], (TILES,), 0, CX * CY), jax.random.fold_in(keys[3], 1), 0, (CX * CY) - 1).astype(jnp.int32)
    owners_keys = jax.random.split(jax.random.fold_in(keys[4], 1), TILES // FT)
    owners_turns = jax.random.permutation(jax.random.fold_in(keys[4], 3), TILES // FT)
    owners = jax.vmap(lambda own, number: shared_out(jax.random.fold_in(keys[4], 2), own, number, FT, N_GX, 1, CAP, 2))(owners_keys, owners_turns).reshape((TILES, 1))
    delays = touch_ends(jax.random.randint(keys[5], (TILES, DIRS), 0, LAG), jax.random.fold_in(keys[5], 1), 0, LAG - 1).astype(jnp.int32)
    weights = scatter_about(keys[6], (2 * CZ, DIRS), (2 * CZ) ** -0.5, 0.375)
    return dict(initial_field=initial_field, inv_permittivity=inv_permittivity, history=history, tile_rows=tile_rows, owners=owners, delays=delays, weights=weights)


courant = 0.5


def curl_upper(padded):
    base = padded[:, :-1, :-1, :-1]
    along_x = padded[:, 1:, :-1, :-1] - base
    along_y = padded[:, :-1, 1:, :-1] - base
    along_z = padded[:, :-1, :-1, 1:] - base
    return jnp.stack([along_y[2] - along_z[1], along_z[0] - along_x[2], along_x[1] - along_y[0]])


def curl_lower(padded):
    base = padded[:, 1:, 1:, 1:]
    along_x = base - padded[:, :-1, 1:, 1:]
    along_y = base - padded[:, 1:, :-1, 1:]
    along_z = base - padded[:, 1:, 1:, :-1]
    return jnp.stack([along_y[2] - along_z[1], along_z[0] - along_x[2], along_x[1] - along_y[0]])


def shifted(proj, delay_block):
    padded = jnp.pad(proj, ((0, 0), (0, NB - HIST), (0, 0)))
    times = lax.broadcasted_iota(jnp.int32, (1, NB, 1), 1)
    where_from = (times - delay_block[:, None, :]) % NB
    return jnp.take_along_axis(padded, where_from, axis=1)


def reference(initial_field, inv_permittivity, history, tile_rows, owners, delays, weights):
    efield = initial_field
    magnetic = jnp.zeros_like(initial_field)
    group = N_GY * N_GZ
    device = jnp.arange(TILES, dtype=jnp.int32) // FT
    block_x = device // group
    block_y = (device // N_GZ) % N_GY
    block_z = device % N_GZ
    global_x = block_x * CX + tile_rows // CY
    global_y = block_y * CY + tile_rows % CY
    samples = []
    for step_index in range(STEPS):
        upper = jnp.pad(efield, ((0, 0), (0, 1), (0, 1), (0, 1)))
        magnetic = magnetic - courant * curl_upper(upper)
        split = magnetic[:2].reshape(2, NX, NY, N_GZ, CZ)
        picked = split[:, global_x, global_y, block_z, :]
        samples.append(jnp.transpose(picked, (1, 0, 2)).reshape(TILES, 2 * CZ))
        lower = jnp.pad(magnetic, ((0, 0), (1, 0), (1, 0), (1, 0)))
        efield = efield + courant * inv_permittivity * curl_lower(lower)
    recent = jnp.stack(samples, axis=1).astype(jnp.bfloat16)
    full_history = jnp.concatenate([history, recent], axis=1)
    weights_wide = weights.astype(jnp.float32)
    blocks = TILES // FT

    def one_block(total, pieces):
        block_history, block_delays, block_owners = pieces
        proj = jnp.einsum('ktf,fd->ktd', block_history.astype(jnp.float32), weights_wide)
        moved = shifted(proj, block_delays)
        return total + jax.ops.segment_sum(moved, block_owners[:, 0], num_segments=N_GX), None

    start = jnp.zeros((N_GX, NB, DIRS), jnp.float32)
    far, _ = lax.scan(one_block, start, (full_history.reshape(blocks, FT, HIST, 2 * CZ), delays.reshape(blocks, FT, DIRS), owners.reshape(blocks, FT, 1)))
    scale = (TILES / N_GX) ** -0.5
    return efield, far * scale
```

```python
import jax
import jax.numpy as jnp
from jax import lax
from jax.experimental import pallas as pl
from jax.experimental.pallas import tpu as pltpu
from jax.sharding import PartitionSpec as P

STEPS = 4
HIST = 16
HPAST = 12
LAG = 4
NB = 20
CAP = 2
W = 4
COURANT = 0.5
MIB = 1 << 20


def pair(low, high, axis):
    count = lax.axis_size(axis)
    up = [(i, i + 1) for i in range(count - 1)]
    down = [(b, a) for a, b in up]
    return lax.ppermute(high, axis, up), lax.ppermute(low, axis, down)


def pack_kernel(e_ref, eps_ref, xlo_ref, xhi_ref, ylo_ref, yhi_ref, full_ref, zlo_ref, zhi_ref):
    nx, ny, nz = e_ref.shape[1:]
    planes = nx + 2 * W
    full_ref[:, 0:W, 0:ny, :] = xlo_ref[...]
    full_ref[0:3, W : W + nx, 0:ny, :] = e_ref[...]
    full_ref[3, W : W + nx, 0:ny, :] = eps_ref[...]
    full_ref[:, W + nx :, 0:ny, :] = xhi_ref[...]
    full_ref[:, :, ny : ny + W, :] = yhi_ref[...]
    full_ref[:, :, ny + W :, :] = ylo_ref[...]
    groups = nz // W
    lane = lax.broadcasted_iota(jnp.int32, (ny + 2 * W, nz), 1)
    for half in range(4 * planes // groups):
        low = jnp.zeros((ny + 2 * W, nz), jnp.float32)
        high = low
        for g in range(groups):
            at = half * groups + g
            plane = full_ref[at // planes, at % planes]
            mine = (lane >= g * W) & (lane < (g + 1) * W)
            low = jnp.where(mine, pltpu.roll(plane, g * W, 1) if g else plane, low)
            high = jnp.where(mine, pltpu.roll(plane, (g + 1) * W, 1) if g + 1 < groups else plane, high)
        zlo_ref[half] = low
        zhi_ref[half] = high


def yee_kernel(
    place_ref, rows_ref, owners_ref, full_ref, zlo_ref, zhi_ref, base_ref,
    out_ref, send_ref, e, h, eps, rec, src, used,
):
    nx, ny, nz = out_ref.shape[1:]
    planes = nx + 2 * W
    tall = ny + 2 * W
    wide = 2 * nz
    tiles = rows_ref.shape[0]
    slots = send_ref.shape[0]
    groups = nz // W
    lane = lax.broadcasted_iota(jnp.int32, (tall, nz), 1)
    for at in range(4 * planes):
        c, p, half, g = at // planes, at % planes, at // groups, at % groups
        up = zhi_ref[half]
        down = zlo_ref[half]
        up = pltpu.roll(up, nz - g * W, 1) if g else up
        down = pltpu.roll(down, nz - (g + 1) * W, 1) if g + 1 < groups else down
        beyond = jnp.where(lane < nz // 2, up, down)
        if c < 3:
            e[c, p, :, 0:nz] = full_ref[c, p]
            e[c, p, :, nz:] = beyond
        else:
            eps[p, :, 0:nz] = COURANT * full_ref[c, p]
            eps[p, :, nz:] = COURANT * beyond
    h[:, 0:W] = jnp.zeros((3, W, tall, wide), jnp.float32)
    row = lax.broadcasted_iota(jnp.int32, (tall, wide), 0)
    col = lax.broadcasted_iota(jnp.int32, (tall, wide), 1)
    outside = ((row >= ny + W) & (place_ref[1] == 0)) | ((col >= wide - W) & (place_ref[2] == 0))
    mask = jnp.where(outside, 0.0, COURANT)

    def yp(a):
        return pltpu.roll(a, tall - 1, 0)

    def ym(a):
        return pltpu.roll(a, 1, 0)

    def zp(a):
        return pltpu.roll(a, wide - 1, 1)

    def zm(a):
        return pltpu.roll(a, 1, 1)

    rec[...] = jnp.zeros(rec.shape, jnp.float32)
    cell = lax.broadcasted_iota(jnp.int32, (tiles, nx * ny), 1)
    pick = (cell == rows_ref[...]).astype(jnp.bfloat16)
    for step in range(STEPS):

        def magnetic(p, _, step=step):
            ex, ey, ez = e[0, p], e[1, p], e[2, p]
            ey1, ez1 = e[1, p + 1], e[2, p + 1]
            cx = mask * ((yp(ez) - ez) - (zp(ey) - ey))
            cy = mask * ((zp(ex) - ex) - (ez1 - ez))
            cz = mask * ((ey1 - ey) - (yp(ex) - ex))
            if step == 0:
                h[0, p], h[1, p], h[2, p] = -cx, -cy, -cz
            else:
                h[0, p], h[1, p], h[2, p] = h[0, p] - cx, h[1, p] - cy, h[2, p] - cz
            return 0

        def electric(p, _):
            hx, hy, hz = h[0, p], h[1, p], h[2, p]
            hy0, hz0 = h[1, p - 1], h[2, p - 1]
            k = eps[p]
            e[0, p] = e[0, p] + k * ((hz - ym(hz)) - (hy - zm(hy)))
            e[1, p] = e[1, p] + k * ((hx - zm(hx)) - (hz - hz0))
            e[2, p] = e[2, p] + k * ((hy - hy0) - (hx - ym(hx)))
            return 0

        first = jnp.where(place_ref[0] == 0, W, step)
        lax.fori_loop(first, planes - 1 - step, magnetic, 0)

        parts = [h[c, W : W + nx, 0:ny, 0:nz].reshape(nx * ny, nz) for c in range(2)]
        inner = jnp.concatenate(parts, axis=1).astype(jnp.bfloat16)
        sample = jnp.dot(pick, inner, preferred_element_type=jnp.float32)
        for k in range(tiles):
            rec[k, HPAST + step : HPAST + step + 1, :] = sample[k : k + 1]
        lax.fori_loop(step + 1, planes - 1 - step, electric, 0)
    out_ref[...] = e[:, W : W + nx, 0:ny, 0:nz]

    def clear_src(i, _):
        src[i] = tiles
        return 0

    def clear_used(i, _):
        used[i] = 0
        return 0

    def assign(k, _):
        owner = owners_ref[k]
        rank = used[owner]
        used[owner] = rank + 1
        src[owner * CAP + rank] = k
        return 0

    lax.fori_loop(0, slots, clear_src, 0)
    lax.fori_loop(0, slots // CAP, clear_used, 0)
    lax.fori_loop(0, tiles, assign, 0)

    def fill(slot, _):
        k = src[slot]

        @pl.when(k < tiles)
        def _():
            send_ref[slot, 0:HIST] = base_ref[k, 0:HIST] + rec[k].astype(jnp.bfloat16)
            send_ref[slot, HIST:] = base_ref[k, HIST:]

        @pl.when(k >= tiles)
        def _():
            send_ref[slot] = jnp.zeros(send_ref.shape[1:], jnp.bfloat16)

        return 0

    lax.fori_loop(0, slots, fill, 0)


def project_kernel(got_ref, weights_ref, out_ref, lag, proj):
    slots = got_ref.shape[0]
    share = weights_ref.shape[1]
    part = pl.program_id(0)

    @pl.when(part == 0)
    def _():
        def widen(k, _):
            wide = got_ref[k, HIST:].astype(jnp.float32)
            lag[k, 0] = wide[:, 0:128]
            lag[k, 1] = wide[:, 128:]
            return 0

        lax.fori_loop(0, slots, widen, 0)

    rows = got_ref[:, 0:HIST, :].reshape(slots * HIST, got_ref.shape[2])
    proj[...] = jnp.dot(rows, weights_ref[...], preferred_element_type=jnp.float32)

    def add(k, sums):
        mine = proj[pl.ds(pl.multiple_of(k * HIST, HIST), HIST), :]
        halves = [jnp.broadcast_to(lag[k, i, pl.ds(part, 1), :], (HIST, 128)) for i in range(2)]
        delay = jnp.concatenate(halves, axis=1)
        return tuple(s + jnp.where(delay == float(j), mine, 0.0) for j, s in enumerate(sums))

    zero = jnp.zeros((HIST, share), jnp.float32)
    sums = lax.fori_loop(0, slots, add, (zero,) * LAG, unroll=4)
    out_ref[0] = jnp.zeros(out_ref.shape[1:], jnp.float32)
    for j in range(LAG):
        out_ref[0, j : j + HIST, :] += sums[j]


def local(initial_field, inv_permittivity, history, tile_rows, owners, delays, weights):
    nx, ny, nz = inv_permittivity.shape
    planes, tall = nx + 2 * W, ny + 2 * W
    tiles = history.shape[0]
    sections = lax.axis_size("gx")
    slots = sections * CAP
    group = lax.axis_size(("gy", "gz"))
    features = history.shape[2]
    share = weights.shape[1] // group
    f32, bf16 = jnp.float32, jnp.bfloat16

    with jax.named_scope("halo"):
        own = inv_permittivity[None]
        xlo, xhi = pair(
            jnp.concatenate([initial_field[:, :W], own[:, :W]]),
            jnp.concatenate([initial_field[:, nx - W :], own[:, nx - W :]]),
            "gx",
        )

        def rows_of(part):
            mid = jnp.concatenate([initial_field[:, :, part], own[:, :, part]])
            return jnp.concatenate([xlo[:, :, part], mid, xhi[:, :, part]], axis=1)

        ylo, yhi = pair(rows_of(slice(0, W)), rows_of(slice(ny - W, ny)), "gy")
        packs = 4 * planes * W // nz
        full, zlo, zhi = pl.pallas_call(
            pack_kernel,
            out_shape=(
                jax.ShapeDtypeStruct((4, planes, tall, nz), f32),
                jax.ShapeDtypeStruct((packs, tall, nz), f32),
                jax.ShapeDtypeStruct((packs, tall, nz), f32),
            ),
            compiler_params=pltpu.CompilerParams(vmem_limit_bytes=16 * MIB),
            name="pack",
        )(initial_field, inv_permittivity, xlo, xhi, ylo, yhi)
        zlo, zhi = pair(zlo, zhi, "gz")

    with jax.named_scope("steps"):
        base = jnp.concatenate(
            [
                jnp.pad(history, ((0, 0), (0, HIST - HPAST), (0, 0))),
                delays.astype(bf16).reshape(tiles, group, share),
            ],
            axis=1,
        )
        place = jnp.stack([lax.axis_index(a) for a in ("gx", "gy", "gz")]).astype(jnp.int32)
        smem = pl.BlockSpec(memory_space=pltpu.SMEM)
        vmem = pl.BlockSpec(memory_space=pltpu.VMEM)
        efield, send = pl.pallas_call(
            yee_kernel,
            out_shape=(
                jax.ShapeDtypeStruct((3, nx, ny, nz), f32),
                jax.ShapeDtypeStruct((slots, HIST + group, features), bf16),
            ),
            in_specs=[smem, vmem, smem] + [vmem] * 4,
            out_specs=(vmem, vmem),
            scratch_shapes=[
                pltpu.VMEM((3, planes, tall, 2 * nz), f32),
                pltpu.VMEM((3, planes, tall, 2 * nz), f32),
                pltpu.VMEM((planes, tall, 2 * nz), f32),
                pltpu.VMEM((tiles, HIST, features), f32),
                pltpu.SMEM((slots,), jnp.int32),
                pltpu.SMEM((sections,), jnp.int32),
            ],
            compiler_params=pltpu.CompilerParams(vmem_limit_bytes=24 * MIB),
            name="yee",
        )(place, tile_rows[:, None], owners[:, 0], full, zlo, zhi, base)

    with jax.named_scope("route"):
        got = lax.all_to_all(send, "gx", split_axis=0, concat_axis=0, tiled=True)

    with jax.named_scope("project"):
        partial = pl.pallas_call(
            project_kernel,
            grid=(group,),
            out_shape=jax.ShapeDtypeStruct((group, 24, share), f32),
            in_specs=[
                pl.BlockSpec((slots, HIST + group, features), lambda i: (0, 0, 0)),
                pl.BlockSpec((features, share), lambda i: (0, i)),
            ],
            out_specs=pl.BlockSpec((1, 24, share), lambda i: (i, 0, 0)),
            scratch_shapes=[
                pltpu.VMEM((slots, 2, group, share // 2), f32),
                pltpu.VMEM((slots * HIST, share), f32),
            ],
            compiler_params=pltpu.CompilerParams(vmem_limit_bytes=24 * MIB),
            name="project",
        )(got, weights)

    with jax.named_scope("far"):
        parts = lax.all_to_all(partial, ("gy", "gz"), split_axis=0, concat_axis=0, tiled=True)
        scale = float(tiles * group) ** (-0.5)
        far = jnp.sum(parts[:, :NB], axis=0) * scale
    return (efield, far[None])


def solution(mesh):
    placed = (
        P(None, "gx", "gy", "gz"),
        P("gx", "gy", "gz"),
        P(("gx", "gy", "gz"), None, None),
        P(("gx", "gy", "gz")),
        P(("gx", "gy", "gz"), None),
        P(("gx", "gy", "gz"), None),
        P(),
    )
    return jax.shard_map(
        local,
        mesh=mesh,
        in_specs=placed,
        out_specs=(P(None, "gx", "gy", "gz"), P("gx", None, ("gy", "gz"))),
        check_vma=False,
    )
```

```python
import jax
import jax.numpy as jnp
from jax import lax
from jax.experimental import pallas as pl
from jax.experimental.pallas import tpu as pltpu
from jax.sharding import PartitionSpec as P

STEPS = 4
HIST = 16
HPAST = 12
LAG = 4
NB = 20
CAP = 2
W = 4
COURANT = 0.5
MIB = 1 << 20


def pair(low, high, axis):
    count = lax.axis_size(axis)
    up = [(i, i + 1) for i in range(count - 1)]
    down = [(b, a) for a, b in up]
    return lax.ppermute(high, axis, up), lax.ppermute(low, axis, down)


def pack_kernel(e_ref, eps_ref, xlo_ref, xhi_ref, ylo_ref, yhi_ref, full_ref, zlo_ref, zhi_ref):
    nx, ny, nz = e_ref.shape[1:]
    planes = nx + 2 * W
    full_ref[:, 0:W, 0:ny, :] = xlo_ref[...]
    full_ref[0:3, W : W + nx, 0:ny, :] = e_ref[...]
    full_ref[3, W : W + nx, 0:ny, :] = eps_ref[...]
    full_ref[:, W + nx :, 0:ny, :] = xhi_ref[...]
    full_ref[:, :, ny : ny + W, :] = yhi_ref[...]
    full_ref[:, :, ny + W :, :] = ylo_ref[...]
    groups = nz // W
    lane = lax.broadcasted_iota(jnp.int32, (ny + 2 * W, nz), 1)
    for half in range(4 * planes // groups):
        low = jnp.zeros((ny + 2 * W, nz), jnp.float32)
        high = low
        for g in range(groups):
            at = half * groups + g
            plane = full_ref[at // planes, at % planes]
            mine = (lane >= g * W) & (lane < (g + 1) * W)
            low = jnp.where(mine, pltpu.roll(plane, g * W, 1) if g else plane, low)
            high = jnp.where(mine, pltpu.roll(plane, (g + 1) * W, 1) if g + 1 < groups else plane, high)
        zlo_ref[half] = low
        zhi_ref[half] = high


def slot_sources(owners_ref, src, used):
    tiles = owners_ref.shape[0]

    def clear_src(i, _):
        src[i] = tiles
        return 0

    def clear_used(i, _):
        used[i] = 0
        return 0

    def assign(k, _):
        owner = owners_ref[k]
        rank = used[owner]
        used[owner] = rank + 1
        src[owner * CAP + rank] = k
        return 0

    lax.fori_loop(0, src.shape[0], clear_src, 0)
    lax.fori_loop(0, used.shape[0], clear_used, 0)
    lax.fori_loop(0, tiles, assign, 0)


def early_kernel(owners_ref, base_ref, send_ref, src, used):
    tiles = owners_ref.shape[0]
    slot_sources(owners_ref, src, used)
    send_ref[...] = jnp.zeros(send_ref.shape, jnp.bfloat16)

    def fill(slot, _):
        k = src[slot]

        @pl.when(k < tiles)
        def _():
            send_ref[slot] = base_ref[k]

        return 0

    lax.fori_loop(0, src.shape[0], fill, 0)


def yee_kernel(
    place_ref, rows_ref, owners_ref, full_ref, zlo_ref, zhi_ref,
    out_ref, send_ref, e, h, eps, rec, src, used,
):
    nx, ny, nz = out_ref.shape[1:]
    planes = nx + 2 * W
    tall = ny + 2 * W
    wide = 2 * nz
    tiles = rows_ref.shape[0]
    slots = send_ref.shape[0]
    groups = nz // W
    lane = lax.broadcasted_iota(jnp.int32, (tall, nz), 1)
    for at in range(4 * planes):
        c, p, half, g = at // planes, at % planes, at // groups, at % groups
        up = zhi_ref[half]
        down = zlo_ref[half]
        up = pltpu.roll(up, nz - g * W, 1) if g else up
        down = pltpu.roll(down, nz - (g + 1) * W, 1) if g + 1 < groups else down
        beyond = jnp.where(lane < nz // 2, up, down)
        if c < 3:
            e[c, p, :, 0:nz] = full_ref[c, p]
            e[c, p, :, nz:] = beyond
        else:
            eps[p, :, 0:nz] = COURANT * full_ref[c, p]
            eps[p, :, nz:] = COURANT * beyond
    h[:, 0:W] = jnp.zeros((3, W, tall, wide), jnp.float32)
    row = lax.broadcasted_iota(jnp.int32, (tall, wide), 0)
    col = lax.broadcasted_iota(jnp.int32, (tall, wide), 1)
    outside = ((row >= ny + W) & (place_ref[1] == 0)) | ((col >= wide - W) & (place_ref[2] == 0))
    mask = jnp.where(outside, 0.0, COURANT)

    def yp(a):
        return pltpu.roll(a, tall - 1, 0)

    def ym(a):
        return pltpu.roll(a, 1, 0)

    def zp(a):
        return pltpu.roll(a, wide - 1, 1)

    def zm(a):
        return pltpu.roll(a, 1, 1)

    cell = lax.broadcasted_iota(jnp.int32, (tiles, nx * ny), 1)
    pick = (cell == rows_ref[...]).astype(jnp.bfloat16)
    for step in range(STEPS):

        def magnetic(p, _, step=step):
            ex, ey, ez = e[0, p], e[1, p], e[2, p]
            ey1, ez1 = e[1, p + 1], e[2, p + 1]
            cx = mask * ((yp(ez) - ez) - (zp(ey) - ey))
            cy = mask * ((zp(ex) - ex) - (ez1 - ez))
            cz = mask * ((ey1 - ey) - (yp(ex) - ex))
            if step == 0:
                h[0, p], h[1, p], h[2, p] = -cx, -cy, -cz
            else:
                h[0, p], h[1, p], h[2, p] = h[0, p] - cx, h[1, p] - cy, h[2, p] - cz
            return 0

        def electric(p, _):
            hx, hy, hz = h[0, p], h[1, p], h[2, p]
            hy0, hz0 = h[1, p - 1], h[2, p - 1]
            k = eps[p]
            e[0, p] = e[0, p] + k * ((hz - ym(hz)) - (hy - zm(hy)))
            e[1, p] = e[1, p] + k * ((hx - zm(hx)) - (hz - hz0))
            e[2, p] = e[2, p] + k * ((hy - hy0) - (hx - ym(hx)))
            return 0

        first = jnp.where(place_ref[0] == 0, W, step)
        lax.fori_loop(first, planes - 1 - step, magnetic, 0)

        parts = [h[c, W : W + nx, 0:ny, 0:nz].reshape(nx * ny, nz) for c in range(2)]
        inner = jnp.concatenate(parts, axis=1).astype(jnp.bfloat16)
        sample = jnp.dot(pick, inner, preferred_element_type=jnp.float32)
        for k in range(tiles):
            rec[k, step : step + 1, :] = sample[k : k + 1]
        lax.fori_loop(step + 1, planes - 1 - step, electric, 0)
    out_ref[...] = e[:, W : W + nx, 0:ny, 0:nz]

    slot_sources(owners_ref, src, used)
    send_ref[...] = jnp.zeros(send_ref.shape, jnp.bfloat16)

    def fill(slot, _):
        k = src[slot]

        @pl.when(k < tiles)
        def _():
            send_ref[slot] = rec[k].astype(jnp.bfloat16)

        return 0

    lax.fori_loop(0, slots, fill, 0)


def sums_of(rows_ref, count, weights, lag, proj, part, slots):
    share = weights.shape[1]
    proj[...] = jnp.dot(rows_ref, weights, preferred_element_type=jnp.float32)

    def add(k, sums):
        mine = proj[pl.ds(pl.multiple_of(k * count, count), count), :]
        halves = [jnp.broadcast_to(lag[k, i, pl.ds(part, 1), :], (count, 128)) for i in range(2)]
        delay = jnp.concatenate(halves, axis=1)
        return tuple(s + jnp.where(delay == float(j), mine, 0.0) for j, s in enumerate(sums))

    zero = jnp.zeros((count, share), jnp.float32)
    return lax.fori_loop(0, slots, add, (zero,) * LAG, unroll=4)


def project_early(got_ref, weights_ref, out_ref, lag_ref, proj):
    slots = got_ref.shape[0]
    part = pl.program_id(0)

    @pl.when(part == 0)
    def _():
        def widen(k, _):
            wide = got_ref[k, HIST:].astype(jnp.float32)
            lag_ref[k, 0] = wide[:, 0:128]
            lag_ref[k, 1] = wide[:, 128:]
            return 0

        lax.fori_loop(0, slots, widen, 0)

    rows = got_ref[:, 0:HIST, :].reshape(slots * HIST, got_ref.shape[2])
    sums = sums_of(rows, HIST, weights_ref[...], lag_ref, proj, part, slots)
    out_ref[0] = jnp.zeros(out_ref.shape[1:], jnp.float32)
    for j in range(LAG):
        out_ref[0, j : j + HIST, :] += sums[j]


def project_late(got_ref, weights_ref, early_ref, lag_ref, out_ref, proj):
    slots = lag_ref.shape[0]
    rows = got_ref[...]
    sums = sums_of(rows, 8, weights_ref[...], lag_ref, proj, pl.program_id(0), slots)
    out_ref[...] = early_ref[...]
    for j in range(LAG):
        out_ref[0, HPAST + j : HIST + j, :] += sums[j][0 : HIST - HPAST]


def local(initial_field, inv_permittivity, history, tile_rows, owners, delays, weights):
    nx, ny, nz = inv_permittivity.shape
    planes, tall = nx + 2 * W, ny + 2 * W
    tiles = history.shape[0]
    sections = lax.axis_size("gx")
    slots = sections * CAP
    group = lax.axis_size(("gy", "gz"))
    features = history.shape[2]
    share = weights.shape[1] // group
    f32, bf16 = jnp.float32, jnp.bfloat16

    smem = pl.BlockSpec(memory_space=pltpu.SMEM)
    vmem = pl.BlockSpec(memory_space=pltpu.VMEM)
    indices = [pltpu.SMEM((slots,), jnp.int32), pltpu.SMEM((sections,), jnp.int32)]
    with jax.named_scope("route_early"):
        base = jnp.concatenate(
            [
                jnp.pad(history, ((0, 0), (0, HIST - HPAST), (0, 0))),
                delays.astype(bf16).reshape(tiles, group, share),
            ],
            axis=1,
        )
        send = pl.pallas_call(
            early_kernel,
            out_shape=jax.ShapeDtypeStruct((slots, HIST + group, features), bf16),
            in_specs=[smem, vmem],
            out_specs=vmem,
            scratch_shapes=indices,
            compiler_params=pltpu.CompilerParams(vmem_limit_bytes=8 * MIB),
            name="early",
        )(owners[:, 0], base)
        got = lax.all_to_all(send, "gx", split_axis=0, concat_axis=0, tiled=True)

    with jax.named_scope("project_early"):
        early, lag = pl.pallas_call(
            project_early,
            grid=(group,),
            out_shape=(
                jax.ShapeDtypeStruct((group, 24, share), f32),
                jax.ShapeDtypeStruct((slots, 2, group, share // 2), f32),
            ),
            in_specs=[
                pl.BlockSpec((slots, HIST + group, features), lambda i: (0, 0, 0)),
                pl.BlockSpec((features, share), lambda i: (0, i)),
            ],
            out_specs=(
                pl.BlockSpec((1, 24, share), lambda i: (i, 0, 0)),
                pl.BlockSpec((slots, 2, group, share // 2), lambda i: (0, 0, 0, 0)),
            ),
            scratch_shapes=[pltpu.VMEM((slots * HIST, share), f32)],
            cost_estimate=pl.CostEstimate(
                flops=2 * slots * HIST * features * share * group, bytes_accessed=30 * MIB, transcendentals=0
            ),
            compiler_params=pltpu.CompilerParams(vmem_limit_bytes=24 * MIB),
            name="project_early",
        )(got, weights)

    with jax.named_scope("halo"):
        own = inv_permittivity[None]
        xlo, xhi = pair(
            jnp.concatenate([initial_field[:, :W], own[:, :W]]),
            jnp.concatenate([initial_field[:, nx - W :], own[:, nx - W :]]),
            "gx",
        )

        def rows_of(part):
            mid = jnp.concatenate([initial_field[:, :, part], own[:, :, part]])
            return jnp.concatenate([xlo[:, :, part], mid, xhi[:, :, part]], axis=1)

        ylo, yhi = pair(rows_of(slice(0, W)), rows_of(slice(ny - W, ny)), "gy")
        packs = 4 * planes * W // nz
        full, zlo, zhi = pl.pallas_call(
            pack_kernel,
            out_shape=(
                jax.ShapeDtypeStruct((4, planes, tall, nz), f32),
                jax.ShapeDtypeStruct((packs, tall, nz), f32),
                jax.ShapeDtypeStruct((packs, tall, nz), f32),
            ),
            compiler_params=pltpu.CompilerParams(vmem_limit_bytes=16 * MIB),
            name="pack",
        )(initial_field, inv_permittivity, xlo, xhi, ylo, yhi)
        zlo, zhi = pair(zlo, zhi, "gz")

    with jax.named_scope("steps"):
        place = jnp.stack([lax.axis_index(a) for a in ("gx", "gy", "gz")]).astype(jnp.int32)
        efield, send = pl.pallas_call(
            yee_kernel,
            out_shape=(
                jax.ShapeDtypeStruct((3, nx, ny, nz), f32),
                jax.ShapeDtypeStruct((slots, HIST - HPAST, features), bf16),
            ),
            in_specs=[smem, vmem, smem] + [vmem] * 3,
            out_specs=(vmem, vmem),
            scratch_shapes=[
                pltpu.VMEM((3, planes, tall, 2 * nz), f32),
                pltpu.VMEM((3, planes, tall, 2 * nz), f32),
                pltpu.VMEM((planes, tall, 2 * nz), f32),
                pltpu.VMEM((tiles, HIST - HPAST, features), f32),
            ]
            + indices,
            compiler_params=pltpu.CompilerParams(vmem_limit_bytes=24 * MIB),
            name="yee",
        )(place, tile_rows[:, None], owners[:, 0], full, zlo, zhi)

    with jax.named_scope("route_late"):
        late = lax.all_to_all(send, "gx", split_axis=0, concat_axis=0, tiled=True)
        late = jnp.pad(late, ((0, 0), (0, 8 - late.shape[1]), (0, 0))).reshape(slots * 8, features)

    with jax.named_scope("project_late"):
        partial = pl.pallas_call(
            project_late,
            grid=(group,),
            out_shape=jax.ShapeDtypeStruct((group, 24, share), f32),
            in_specs=[
                pl.BlockSpec((slots * 8, features), lambda i: (0, 0)),
                pl.BlockSpec((features, share), lambda i: (0, i)),
                pl.BlockSpec((1, 24, share), lambda i: (i, 0, 0)),
                pl.BlockSpec((slots, 2, group, share // 2), lambda i: (0, 0, 0, 0)),
            ],
            out_specs=pl.BlockSpec((1, 24, share), lambda i: (i, 0, 0)),
            scratch_shapes=[pltpu.VMEM((slots * 8, share), f32)],
            compiler_params=pltpu.CompilerParams(vmem_limit_bytes=24 * MIB),
            name="project_late",
        )(late, weights, early, lag)

    with jax.named_scope("far"):
        parts = lax.all_to_all(partial, ("gy", "gz"), split_axis=0, concat_axis=0, tiled=True)
        scale = float(tiles * group) ** (-0.5)
        far = jnp.sum(parts[:, :NB], axis=0) * scale
    return (efield, far[None])


def solution(mesh):
    placed = (
        P(None, "gx", "gy", "gz"),
        P("gx", "gy", "gz"),
        P(("gx", "gy", "gz"), None, None),
        P(("gx", "gy", "gz")),
        P(("gx", "gy", "gz"), None),
        P(("gx", "gy", "gz"), None),
        P(),
    )
    return jax.shard_map(
        local,
        mesh=mesh,
        in_specs=placed,
        out_specs=(P(None, "gx", "gy", "gz"), P("gx", None, ("gy", "gz"))),
        check_vma=False,
    )
```

```python
import jax
import jax.numpy as jnp
from jax import lax
from jax.experimental import pallas as pl
from jax.experimental.pallas import tpu as pltpu
from jax.sharding import PartitionSpec as P

STEPS = 4
HIST = 16
HPAST = 12
LAG = 4
NB = 20
CAP = 2
W = 4
COURANT = 0.5
MIB = 1 << 20


def pair(low, high, axis):
    count = lax.axis_size(axis)
    up = [(i, i + 1) for i in range(count - 1)]
    down = [(b, a) for a, b in up]
    return lax.ppermute(high, axis, up), lax.ppermute(low, axis, down)


def pack_kernel(e_ref, eps_ref, xlo_ref, xhi_ref, ylo_ref, yhi_ref, full_ref, zlo_ref, zhi_ref):
    nx, ny, nz = e_ref.shape[1:]
    planes = nx + 2 * W
    full_ref[:, 0:W, 0:ny, :] = xlo_ref[...]
    full_ref[0:3, W : W + nx, 0:ny, :] = e_ref[...]
    full_ref[3, W : W + nx, 0:ny, :] = eps_ref[...]
    full_ref[:, W + nx :, 0:ny, :] = xhi_ref[...]
    full_ref[:, :, ny : ny + W, :] = yhi_ref[...]
    full_ref[:, :, ny + W :, :] = ylo_ref[...]
    groups = nz // W
    lane = lax.broadcasted_iota(jnp.int32, (ny + 2 * W, nz), 1)
    for half in range(4 * planes // groups):
        low = jnp.zeros((ny + 2 * W, nz), jnp.float32)
        high = low
        for g in range(groups):
            at = half * groups + g
            plane = full_ref[at // planes, at % planes]
            mine = (lane >= g * W) & (lane < (g + 1) * W)
            low = jnp.where(mine, pltpu.roll(plane, g * W, 1) if g else plane, low)
            high = jnp.where(mine, pltpu.roll(plane, (g + 1) * W, 1) if g + 1 < groups else plane, high)
        zlo_ref[half] = low
        zhi_ref[half] = high


def slot_sources(owners_ref, src, used):
    tiles = owners_ref.shape[0]

    def clear_src(i, _):
        src[i] = tiles
        return 0

    def clear_used(i, _):
        used[i] = 0
        return 0

    def assign(k, _):
        owner = owners_ref[k]
        rank = used[owner]
        used[owner] = rank + 1
        src[owner * CAP + rank] = k
        return 0

    lax.fori_loop(0, src.shape[0], clear_src, 0)
    lax.fori_loop(0, used.shape[0], clear_used, 0)
    lax.fori_loop(0, tiles, assign, 0)


def early_kernel(owners_ref, base_ref, send_ref, src, used):
    tiles = owners_ref.shape[0]
    slot_sources(owners_ref, src, used)
    send_ref[...] = jnp.zeros(send_ref.shape, jnp.bfloat16)

    def fill(slot, _):
        k = src[slot]

        @pl.when(k < tiles)
        def _():
            send_ref[slot] = base_ref[k]

        return 0

    lax.fori_loop(0, src.shape[0], fill, 0)


def yee_kernel(
    place_ref, rows_ref, owners_ref, full_ref, zlo_ref, zhi_ref, after_ref,
    out_ref, send_ref, e, h, eps, rec, src, used,
):
    del after_ref
    nx, ny, nz = out_ref.shape[1:]
    planes = nx + 2 * W
    tall = ny + 2 * W
    wide = 2 * nz
    tiles = rows_ref.shape[0]
    slots = send_ref.shape[0]
    groups = nz // W
    lane = lax.broadcasted_iota(jnp.int32, (tall, nz), 1)
    for at in range(4 * planes):
        c, p, half, g = at // planes, at % planes, at // groups, at % groups
        up = zhi_ref[half]
        down = zlo_ref[half]
        up = pltpu.roll(up, nz - g * W, 1) if g else up
        down = pltpu.roll(down, nz - (g + 1) * W, 1) if g + 1 < groups else down
        beyond = jnp.where(lane < nz // 2, up, down)
        if c < 3:
            e[c, p, :, 0:nz] = full_ref[c, p]
            e[c, p, :, nz:] = beyond
        else:
            eps[p, :, 0:nz] = COURANT * full_ref[c, p]
            eps[p, :, nz:] = COURANT * beyond
    h[:, 0:W] = jnp.zeros((3, W, tall, wide), jnp.float32)
    row = lax.broadcasted_iota(jnp.int32, (tall, wide), 0)
    col = lax.broadcasted_iota(jnp.int32, (tall, wide), 1)
    outside = ((row >= ny + W) & (place_ref[1] == 0)) | ((col >= wide - W) & (place_ref[2] == 0))
    mask = jnp.where(outside, 0.0, COURANT)

    def yp(a):
        return pltpu.roll(a, tall - 1, 0)

    def ym(a):
        return pltpu.roll(a, 1, 0)

    def zp(a):
        return pltpu.roll(a, wide - 1, 1)

    def zm(a):
        return pltpu.roll(a, 1, 1)

    cell = lax.broadcasted_iota(jnp.int32, (tiles, nx * ny), 1)
    pick = (cell == rows_ref[...]).astype(jnp.bfloat16)
    for step in range(STEPS):

        def magnetic(p, _, step=step):
            ex, ey, ez = e[0, p], e[1, p], e[2, p]
            ey1, ez1 = e[1, p + 1], e[2, p + 1]
            cx = mask * ((yp(ez) - ez) - (zp(ey) - ey))
            cy = mask * ((zp(ex) - ex) - (ez1 - ez))
            cz = mask * ((ey1 - ey) - (yp(ex) - ex))
            if step == 0:
                h[0, p], h[1, p], h[2, p] = -cx, -cy, -cz
            else:
                h[0, p], h[1, p], h[2, p] = h[0, p] - cx, h[1, p] - cy, h[2, p] - cz
            return 0

        def electric(p, _):
            hx, hy, hz = h[0, p], h[1, p], h[2, p]
            hy0, hz0 = h[1, p - 1], h[2, p - 1]
            k = eps[p]
            e[0, p] = e[0, p] + k * ((hz - ym(hz)) - (hy - zm(hy)))
            e[1, p] = e[1, p] + k * ((hx - zm(hx)) - (hz - hz0))
            e[2, p] = e[2, p] + k * ((hy - hy0) - (hx - ym(hx)))
            return 0

        first = jnp.where(place_ref[0] == 0, W, step)
        lax.fori_loop(first, planes - 1 - step, magnetic, 0)

        parts = [h[c, W : W + nx, 0:ny, 0:nz].reshape(nx * ny, nz) for c in range(2)]
        inner = jnp.concatenate(parts, axis=1).astype(jnp.bfloat16)
        sample = jnp.dot(pick, inner, preferred_element_type=jnp.float32)
        for k in range(tiles):
            rec[k, step : step + 1, :] = sample[k : k + 1]
        lax.fori_loop(step + 1, planes - 1 - step, electric, 0)
    out_ref[...] = e[:, W : W + nx, 0:ny, 0:nz]

    slot_sources(owners_ref, src, used)
    send_ref[...] = jnp.zeros(send_ref.shape, jnp.bfloat16)

    def fill(slot, _):
        k = src[slot]

        @pl.when(k < tiles)
        def _():
            send_ref[slot] = rec[k].astype(jnp.bfloat16)

        return 0

    lax.fori_loop(0, slots, fill, 0)


def sums_of(rows_ref, count, weights, lag, proj, part, slots):
    share = weights.shape[1]
    proj[...] = jnp.dot(rows_ref, weights, preferred_element_type=jnp.float32)

    def add(k, sums):
        mine = proj[pl.ds(pl.multiple_of(k * count, count), count), :]
        halves = [jnp.broadcast_to(lag[k, i, pl.ds(part, 1), :], (count, 128)) for i in range(2)]
        delay = jnp.concatenate(halves, axis=1)
        return tuple(s + jnp.where(delay == float(j), mine, 0.0) for j, s in enumerate(sums))

    zero = jnp.zeros((count, share), jnp.float32)
    return lax.fori_loop(0, slots, add, (zero,) * LAG, unroll=4)


def project_early(got_ref, weights_ref, out_ref, lag_ref, proj):
    slots = got_ref.shape[0]
    part = pl.program_id(0)

    @pl.when(part == 0)
    def _():
        def widen(k, _):
            wide = got_ref[k, HIST:].astype(jnp.float32)
            lag_ref[k, 0] = wide[:, 0:128]
            lag_ref[k, 1] = wide[:, 128:]
            return 0

        lax.fori_loop(0, slots, widen, 0)

    rows = got_ref[:, 0:HIST, :].reshape(slots * HIST, got_ref.shape[2])
    sums = sums_of(rows, HIST, weights_ref[...], lag_ref, proj, part, slots)
    out_ref[0] = jnp.zeros(out_ref.shape[1:], jnp.float32)
    for j in range(LAG):
        out_ref[0, j : j + HIST, :] += sums[j]


def project_late(got_ref, weights_ref, early_ref, lag_ref, out_ref, proj):
    slots = lag_ref.shape[0]
    rows = got_ref[...]
    sums = sums_of(rows, 8, weights_ref[...], lag_ref, proj, pl.program_id(0), slots)
    out_ref[...] = early_ref[...]
    for j in range(LAG):
        out_ref[0, HPAST + j : HIST + j, :] += sums[j][0 : HIST - HPAST]


def local(initial_field, inv_permittivity, history, tile_rows, owners, delays, weights):
    nx, ny, nz = inv_permittivity.shape
    planes, tall = nx + 2 * W, ny + 2 * W
    tiles = history.shape[0]
    sections = lax.axis_size("gx")
    slots = sections * CAP
    group = lax.axis_size(("gy", "gz"))
    features = history.shape[2]
    share = weights.shape[1] // group
    f32, bf16 = jnp.float32, jnp.bfloat16

    smem = pl.BlockSpec(memory_space=pltpu.SMEM)
    vmem = pl.BlockSpec(memory_space=pltpu.VMEM)
    indices = [pltpu.SMEM((slots,), jnp.int32), pltpu.SMEM((sections,), jnp.int32)]
    with jax.named_scope("route_early"):
        base = jnp.concatenate(
            [
                jnp.pad(history, ((0, 0), (0, HIST - HPAST), (0, 0))),
                delays.astype(bf16).reshape(tiles, group, share),
            ],
            axis=1,
        )
        send = pl.pallas_call(
            early_kernel,
            out_shape=jax.ShapeDtypeStruct((slots, HIST + group, features), bf16),
            in_specs=[smem, vmem],
            out_specs=vmem,
            scratch_shapes=indices,
            compiler_params=pltpu.CompilerParams(vmem_limit_bytes=8 * MIB),
            name="early",
        )(owners[:, 0], base)
        got = lax.all_to_all(send, "gx", split_axis=0, concat_axis=0, tiled=True)

    with jax.named_scope("project_early"):
        early, lag = pl.pallas_call(
            project_early,
            grid=(group,),
            out_shape=(
                jax.ShapeDtypeStruct((group, 24, share), f32),
                jax.ShapeDtypeStruct((slots, 2, group, share // 2), f32),
            ),
            in_specs=[
                pl.BlockSpec((slots, HIST + group, features), lambda i: (0, 0, 0)),
                pl.BlockSpec((features, share), lambda i: (0, i)),
            ],
            out_specs=(
                pl.BlockSpec((1, 24, share), lambda i: (i, 0, 0)),
                pl.BlockSpec((slots, 2, group, share // 2), lambda i: (0, 0, 0, 0)),
            ),
            scratch_shapes=[pltpu.VMEM((slots * HIST, share), f32)],
            cost_estimate=pl.CostEstimate(
                flops=2 * slots * HIST * features * share * group, bytes_accessed=30 * MIB, transcendentals=0
            ),
            compiler_params=pltpu.CompilerParams(vmem_limit_bytes=24 * MIB),
            name="project_early",
        )(got, weights)

    with jax.named_scope("halo"):
        own = inv_permittivity[None]
        xlo, xhi = pair(
            jnp.concatenate([initial_field[:, :W], own[:, :W]]),
            jnp.concatenate([initial_field[:, nx - W :], own[:, nx - W :]]),
            "gx",
        )

        def rows_of(part):
            mid = jnp.concatenate([initial_field[:, :, part], own[:, :, part]])
            return jnp.concatenate([xlo[:, :, part], mid, xhi[:, :, part]], axis=1)

        ylo, yhi = pair(rows_of(slice(0, W)), rows_of(slice(ny - W, ny)), "gy")
        packs = 4 * planes * W // nz
        full, zlo, zhi = pl.pallas_call(
            pack_kernel,
            out_shape=(
                jax.ShapeDtypeStruct((4, planes, tall, nz), f32),
                jax.ShapeDtypeStruct((packs, tall, nz), f32),
                jax.ShapeDtypeStruct((packs, tall, nz), f32),
            ),
            compiler_params=pltpu.CompilerParams(vmem_limit_bytes=16 * MIB),
            name="pack",
        )(initial_field, inv_permittivity, xlo, xhi, ylo, yhi)
        zlo, zhi = pair(zlo, zhi, "gz")

    with jax.named_scope("steps"):
        place = jnp.stack([lax.axis_index(a) for a in ("gx", "gy", "gz")]).astype(jnp.int32)
        efield, send = pl.pallas_call(
            yee_kernel,
            out_shape=(
                jax.ShapeDtypeStruct((3, nx, ny, nz), f32),
                jax.ShapeDtypeStruct((slots, HIST - HPAST, features), bf16),
            ),
            in_specs=[smem, vmem, smem] + [vmem] * 3 + [pl.BlockSpec(memory_space=pl.ANY)],
            out_specs=(vmem, vmem),
            scratch_shapes=[
                pltpu.VMEM((3, planes, tall, 2 * nz), f32),
                pltpu.VMEM((3, planes, tall, 2 * nz), f32),
                pltpu.VMEM((planes, tall, 2 * nz), f32),
                pltpu.VMEM((tiles, HIST - HPAST, features), f32),
            ]
            + indices,
            compiler_params=pltpu.CompilerParams(vmem_limit_bytes=24 * MIB),
            name="yee",
        )(place, tile_rows[:, None], owners[:, 0], full, zlo, zhi, got)

    with jax.named_scope("route_late"):
        late = lax.all_to_all(send, "gx", split_axis=0, concat_axis=0, tiled=True)
        late = jnp.pad(late, ((0, 0), (0, 8 - late.shape[1]), (0, 0))).reshape(slots * 8, features)

    with jax.named_scope("project_late"):
        partial = pl.pallas_call(
            project_late,
            grid=(group,),
            out_shape=jax.ShapeDtypeStruct((group, 24, share), f32),
            in_specs=[
                pl.BlockSpec((slots * 8, features), lambda i: (0, 0)),
                pl.BlockSpec((features, share), lambda i: (0, i)),
                pl.BlockSpec((1, 24, share), lambda i: (i, 0, 0)),
                pl.BlockSpec((slots, 2, group, share // 2), lambda i: (0, 0, 0, 0)),
            ],
            out_specs=pl.BlockSpec((1, 24, share), lambda i: (i, 0, 0)),
            scratch_shapes=[pltpu.VMEM((slots * 8, share), f32)],
            compiler_params=pltpu.CompilerParams(vmem_limit_bytes=24 * MIB),
            name="project_late",
        )(late, weights, early, lag)

    with jax.named_scope("far"):
        parts = lax.all_to_all(partial, ("gy", "gz"), split_axis=0, concat_axis=0, tiled=True)
        scale = float(tiles * group) ** (-0.5)
        far = jnp.sum(parts[:, :NB], axis=0) * scale
    return (efield, far[None])


def solution(mesh):
    placed = (
        P(None, "gx", "gy", "gz"),
        P("gx", "gy", "gz"),
        P(("gx", "gy", "gz"), None, None),
        P(("gx", "gy", "gz")),
        P(("gx", "gy", "gz"), None),
        P(("gx", "gy", "gz"), None),
        P(),
    )
    return jax.shard_map(
        local,
        mesh=mesh,
        in_specs=placed,
        out_specs=(P(None, "gx", "gy", "gz"), P("gx", None, ("gy", "gz"))),
        check_vma=False,
    )
```

```python
import functools

import jax
import jax.numpy as jnp
from jax import lax
from jax.experimental import pallas as pl
from jax.experimental.pallas import tpu as pltpu
from jax.sharding import PartitionSpec as P

STEPS = 4
HIST = 16
HPAST = 12
LAG = 4
NB = 20
CAP = 2
W = 4
COURANT = 0.5
MIB = 1 << 20


def pair(low, high, axis):
    count = lax.axis_size(axis)
    up = [(i, i + 1) for i in range(count - 1)]
    down = [(b, a) for a, b in up]
    return lax.ppermute(high, axis, up), lax.ppermute(low, axis, down)


def assemble(e_ref, eps_ref, xlo_ref, xhi_ref, ylo_ref, yhi_ref, full_ref):
    nx, ny = e_ref.shape[1:3]
    full_ref[:, 0:W, 0:ny, :] = xlo_ref[...]
    full_ref[0:3, W : W + nx, 0:ny, :] = e_ref[...]
    full_ref[3, W : W + nx, 0:ny, :] = eps_ref[...]
    full_ref[:, W + nx :, 0:ny, :] = xhi_ref[...]
    full_ref[:, :, ny : ny + W, :] = yhi_ref[...]
    full_ref[:, :, ny + W :, :] = ylo_ref[...]


def pack_kernel(e_ref, eps_ref, xlo_ref, xhi_ref, ylo_ref, yhi_ref, zlo_ref, zhi_ref, full_ref):
    nx, ny, nz = e_ref.shape[1:]
    planes = nx + 2 * W
    assemble(e_ref, eps_ref, xlo_ref, xhi_ref, ylo_ref, yhi_ref, full_ref)
    groups = nz // W
    lane = lax.broadcasted_iota(jnp.int32, (ny + 2 * W, nz), 1)
    for half in range(4 * planes // groups):
        low = jnp.zeros((ny + 2 * W, nz), jnp.float32)
        high = low
        for g in range(groups):
            at = half * groups + g
            plane = full_ref[at // planes, at % planes]
            mine = (lane >= g * W) & (lane < (g + 1) * W)
            low = jnp.where(mine, pltpu.roll(plane, g * W, 1) if g else plane, low)
            high = jnp.where(mine, pltpu.roll(plane, (g + 1) * W, 1) if g + 1 < groups else plane, high)
        zlo_ref[half] = low
        zhi_ref[half] = high


def slot_sources(owners_ref, src, used):
    tiles = owners_ref.shape[0]

    def clear_src(i, _):
        src[i] = tiles
        return 0

    def clear_used(i, _):
        used[i] = 0
        return 0

    def assign(k, _):
        owner = owners_ref[k]
        rank = used[owner]
        used[owner] = rank + 1
        src[owner * CAP + rank] = k
        return 0

    lax.fori_loop(0, src.shape[0], clear_src, 0)
    lax.fori_loop(0, used.shape[0], clear_used, 0)
    lax.fori_loop(0, tiles, assign, 0)


def early_kernel(owners_ref, past_ref, delays_ref, send_ref, src, used):
    slot_sources(owners_ref, src, used)
    for s in range(send_ref.shape[0]):
        first, second = src[CAP * s], src[CAP * s + 1]
        send_ref[s, 0:32] = past_ref[0, first] + past_ref[1, second]
        send_ref[s, 32:48] = delays_ref[first]
        send_ref[s, 48:64] = delays_ref[second]


def yee_kernel(
    place_ref, rows_ref, owners_ref, e_ref, eps_ref, xlo_ref, xhi_ref, ylo_ref, yhi_ref, zlo_ref, zhi_ref,
    out_ref, send_ref, full, e, h, eps, rec, src, used,
):
    assemble(e_ref, eps_ref, xlo_ref, xhi_ref, ylo_ref, yhi_ref, full)
    nx, ny, nz = out_ref.shape[1:]
    planes = nx + 2 * W
    tall = ny + 2 * W
    wide = 2 * nz
    tiles = rows_ref.shape[0]
    groups = nz // W
    lane = lax.broadcasted_iota(jnp.int32, (tall, nz), 1)
    for at in range(4 * planes):
        c, p, half, g = at // planes, at % planes, at // groups, at % groups
        up = zhi_ref[half]
        down = zlo_ref[half]
        up = pltpu.roll(up, nz - g * W, 1) if g else up
        down = pltpu.roll(down, nz - (g + 1) * W, 1) if g + 1 < groups else down
        beyond = jnp.where(lane < nz // 2, up, down)
        if c < 3:
            e[c, p, :, 0:nz] = full[c, p]
            e[c, p, :, nz:] = beyond
        else:
            eps[p, :, 0:nz] = COURANT * full[c, p]
            eps[p, :, nz:] = COURANT * beyond
    row = lax.broadcasted_iota(jnp.int32, (tall, wide), 0)
    col = lax.broadcasted_iota(jnp.int32, (tall, wide), 1)
    outside = ((row >= ny + W) & (place_ref[1] == 0)) | ((col >= wide - W) & (place_ref[2] == 0))
    mask = jnp.where(outside, 0.0, COURANT)

    def yp(a):
        return pltpu.roll(a, tall - 1, 0)

    def ym(a):
        return pltpu.roll(a, 1, 0)

    def zp(a):
        return pltpu.roll(a, wide - 1, 1)

    def zm(a):
        return pltpu.roll(a, 1, 1)

    rec[...] = jnp.zeros(rec.shape, jnp.float32)
    cell = lax.broadcasted_iota(jnp.int32, (tiles, nx * ny), 1)
    pick = (cell == rows_ref[...]).astype(jnp.bfloat16)
    for step in range(STEPS):

        def magnetic(p, _, step=step):
            ex, ey, ez = e[0, p], e[1, p], e[2, p]
            ey1, ez1 = e[1, p + 1], e[2, p + 1]
            cx = mask * ((yp(ez) - ez) - (zp(ey) - ey))
            cy = mask * ((zp(ex) - ex) - (ez1 - ez))
            cz = mask * ((ey1 - ey) - (yp(ex) - ex))
            if step == 0:
                h[0, p], h[1, p], h[2, p] = -cx, -cy, -cz
            else:
                h[0, p], h[1, p], h[2, p] = h[0, p] - cx, h[1, p] - cy, h[2, p] - cz
            return 0

        def electric(p, _):
            hx, hy, hz = h[0, p], h[1, p], h[2, p]
            hy0, hz0 = h[1, p - 1], h[2, p - 1]
            k = eps[p]
            e[0, p] = e[0, p] + k * ((hz - ym(hz)) - (hy - zm(hy)))
            e[1, p] = e[1, p] + k * ((hx - zm(hx)) - (hz - hz0))
            e[2, p] = e[2, p] + k * ((hy - hy0) - (hx - ym(hx)))
            return 0

        lax.fori_loop(step, planes - 1 - step, magnetic, 0, unroll=4)

        @pl.when(place_ref[0] == 0)
        def _():
            h[:, W - 1] = jnp.zeros((3, tall, wide), jnp.float32)


        parts = [h[c, W : W + nx, 0:ny, 0:nz].reshape(nx * ny, nz) for c in range(2)]
        inner = jnp.concatenate(parts, axis=1).astype(jnp.bfloat16)
        sample = jnp.dot(pick, inner, preferred_element_type=jnp.float32)
        for k in range(tiles):
            for half in range(CAP):
                at = half * (HIST - HPAST) + step
                rec[half, k, at : at + 1, :] = sample[k : k + 1]
        lax.fori_loop(step + 1, planes - 1 - step, electric, 0, unroll=4)
    out_ref[...] = e[:, W : W + nx, 0:ny, 0:nz]

    slot_sources(owners_ref, src, used)
    for s in range(send_ref.shape[0]):
        both = rec[0, src[CAP * s]] + rec[1, src[CAP * s + 1]]
        send_ref[s] = both.astype(jnp.bfloat16)


def delays_of(lag, slot, part):
    rows = [jnp.broadcast_to(lag[slot, i, pl.ds(part, 1), :], (8, lag.shape[3])) for i in range(2)]
    return jnp.concatenate(rows, axis=1)


def add_delayed(sums, values, delay):
    for j in range(1, LAG):
        sums[j - 1] = sums[j - 1] + jnp.where(delay == float(j), values, 0.0)


def split3(total, pieces_ref):
    rows = total.shape[0]
    for i in range(3):
        piece = total.astype(jnp.bfloat16)
        pieces_ref[rows * i : rows * (i + 1)] = piece
        total = total - piece.astype(jnp.float32)


def project_total(pieces_ref, weights):
    parts = jnp.dot(pieces_ref[...], weights, preferred_element_type=jnp.float32)
    rows = parts.shape[0] // 3
    return parts[0:rows] + parts[rows : 2 * rows] + parts[2 * rows :]


def project_early(got_ref, weights_ref, out_ref, lag_ref, pieces):
    pairs, _, features = got_ref.shape
    share = weights_ref.shape[1]
    part = pl.program_id(0)

    @pl.when(part == 0)
    def _():
        def widen(s, total):
            for i in range(CAP):
                wide = got_ref[s, 32 + 16 * i : 48 + 16 * i].astype(jnp.float32)
                lag_ref[CAP * s + i, 0] = wide[:, 0 : share // 2]
                lag_ref[CAP * s + i, 1] = wide[:, share // 2 :]
            return total + got_ref[s, 0:32].astype(jnp.float32)

        total = lax.fori_loop(0, pairs, widen, jnp.zeros((32, features), jnp.float32), unroll=4)
        split3(total, pieces)

    weights = weights_ref[...]
    total = project_total(pieces, weights)
    upper = lax.broadcasted_iota(jnp.int32, (8, share), 0) < HPAST - 8
    low = [jnp.zeros((8, share), jnp.float32)] * (LAG - 1)
    high = list(low)
    block = min(8, pairs)
    for b in range(0, pairs, block):
        rows = got_ref[b : b + block, 0:32, :].reshape(block * 32, features)
        proj = jnp.dot(rows, weights, preferred_element_type=jnp.float32)
        for s in range(block):
            first = delays_of(lag_ref, CAP * (b + s), part)
            second = delays_of(lag_ref, CAP * (b + s) + 1, part)
            add_delayed(low, proj[32 * s : 32 * s + 8], first)
            add_delayed(low, proj[32 * s + 8 : 32 * s + 16], second)
            add_delayed(high, proj[32 * s + 16 : 32 * s + 24], jnp.where(upper, first, second))
    low.insert(0, total[0:8] + total[8:16] - low[0] - low[1] - low[2])
    high.insert(0, total[16:24] - high[0] - high[1] - high[2])
    out_ref[0] = jnp.zeros(out_ref.shape[1:], jnp.float32)
    for j in range(LAG):
        out_ref[0, j : j + 8, :] += low[j]
        out_ref[0, j + 8 : j + HPAST, :] += high[j][0:4] + high[j][4:8]


def project_late(got_ref, weights_ref, early_ref, lag_ref, out_ref, pieces, bins):
    pairs = got_ref.shape[0] // 8
    share = weights_ref.shape[1]
    part = pl.program_id(0)

    @pl.when(part == 0)
    def _():
        wide = got_ref[...].astype(jnp.float32)
        total = wide[0:8]
        for s in range(1, pairs):
            total = total + wide[8 * s : 8 * s + 8]
        split3(jnp.concatenate([total, jnp.zeros_like(total)]), pieces)

    weights = weights_ref[...]
    total = project_total(pieces, weights)[0:8]
    proj = jnp.dot(got_ref[...], weights, preferred_element_type=jnp.float32)
    upper = lax.broadcasted_iota(jnp.int32, (8, share), 0) < HIST - HPAST
    sums = [jnp.zeros((8, share), jnp.float32)] * (LAG - 1)
    for s in range(pairs):
        delay = jnp.where(upper, delays_of(lag_ref, CAP * s, part), delays_of(lag_ref, CAP * s + 1, part))
        add_delayed(sums, proj[8 * s : 8 * s + 8], delay)
    sums.insert(0, total - sums[0] - sums[1] - sums[2])
    bins[...] = early_ref[0]
    for j in range(LAG):
        bins[HPAST + j : HIST + j, :] += sums[j][0:4] + sums[j][4:8]
    for i in range(2):
        out_ref[0, NB * i : NB * (i + 1), :] = bins[0:NB, share // 2 * i : share // 2 * (i + 1)]


def sum_kernel(parts_ref, out_ref, *, scale):
    half = parts_ref.shape[2]
    total = jnp.sum(parts_ref[...], axis=0) * scale
    for i in range(2):
        out_ref[0, :, half * i : half * (i + 1)] = total[NB * i : NB * (i + 1)]


def local(initial_field, inv_permittivity, history, tile_rows, owners, delays, weights):
    nx, ny, nz = inv_permittivity.shape
    planes, tall = nx + 2 * W, ny + 2 * W
    tiles = history.shape[0]
    sections = lax.axis_size("gx")
    slots = sections * CAP
    group = lax.axis_size(("gy", "gz"))
    features = history.shape[2]
    share = weights.shape[1] // group
    f32, bf16 = jnp.float32, jnp.bfloat16

    smem = pl.BlockSpec(memory_space=pltpu.SMEM)
    vmem = pl.BlockSpec(memory_space=pltpu.VMEM)
    indices = [pltpu.SMEM((slots,), jnp.int32), pltpu.SMEM((sections,), jnp.int32)]
    with jax.named_scope("halo"):
        own = inv_permittivity[None]
        xlo, xhi = pair(
            jnp.concatenate([initial_field[:, :W], own[:, :W]]),
            jnp.concatenate([initial_field[:, nx - W :], own[:, nx - W :]]),
            "gx",
        )

        def rows_of(part):
            mid = jnp.concatenate([initial_field[:, :, part], own[:, :, part]])
            return jnp.concatenate([xlo[:, :, part], mid, xhi[:, :, part]], axis=1)

        ylo, yhi = pair(rows_of(slice(0, W)), rows_of(slice(ny - W, ny)), "gy")
        packs = 4 * planes * W // nz
        zlo, zhi = pl.pallas_call(
            pack_kernel,
            out_shape=(
                jax.ShapeDtypeStruct((packs, tall, nz), f32),
                jax.ShapeDtypeStruct((packs, tall, nz), f32),
            ),
            scratch_shapes=[pltpu.VMEM((4, planes, tall, nz), f32)],
            compiler_params=pltpu.CompilerParams(vmem_limit_bytes=16 * MIB),
            name="pack",
        )(initial_field, inv_permittivity, xlo, xhi, ylo, yhi)
        zlo, zhi = pair(zlo, zhi, "gz")

    with jax.named_scope("route_early"):
        extra = ((0, 1), (0, 0), (0, 0))
        past = jnp.pad(history, extra)

        def gap(rows):
            return jnp.zeros((tiles + 1, rows, features), bf16)

        low, high = past[:, 0:8], past[:, 8:HPAST]
        past = jnp.stack(
            [
                jnp.concatenate([low, gap(8), high, gap(12)], axis=1),
                jnp.concatenate([gap(8), low, gap(4), high, gap(8)], axis=1),
            ]
        )
        lags = jnp.pad(delays.astype(bf16).reshape(tiles, group, share), extra)
        send = pl.pallas_call(
            early_kernel,
            out_shape=jax.ShapeDtypeStruct((sections, 32 + CAP * group, features), bf16),
            in_specs=[smem, vmem, vmem],
            out_specs=vmem,
            scratch_shapes=indices,
            compiler_params=pltpu.CompilerParams(vmem_limit_bytes=8 * MIB),
            name="early",
        )(owners[:, 0], past, lags)
        send, _, _ = lax.optimization_barrier((send, xlo, xhi))
        got = lax.all_to_all(send, "gx", split_axis=0, concat_axis=0, tiled=True)

    with jax.named_scope("project_early"):
        early, lag = pl.pallas_call(
            project_early,
            grid=(group,),
            out_shape=(
                jax.ShapeDtypeStruct((group, 24, share), f32),
                jax.ShapeDtypeStruct((slots, 2, group, share // 2), f32),
            ),
            in_specs=[
                pl.BlockSpec((sections, 32 + CAP * group, features), lambda i: (0, 0, 0)),
                pl.BlockSpec((features, share), lambda i: (0, i)),
            ],
            out_specs=(
                pl.BlockSpec((1, 24, share), lambda i: (i, 0, 0)),
                pl.BlockSpec((slots, 2, group, share // 2), lambda i: (0, 0, 0, 0)),
            ),
            scratch_shapes=[pltpu.VMEM((3 * 32, features), bf16)],
            cost_estimate=pl.CostEstimate(
                flops=2 * slots * HIST * features * share * group, bytes_accessed=30 * MIB, transcendentals=0
            ),
            compiler_params=pltpu.CompilerParams(vmem_limit_bytes=24 * MIB),
            name="project_early",
        )(got, weights)

    with jax.named_scope("steps"):
        place = jnp.stack([lax.axis_index(a) for a in ("gx", "gy", "gz")]).astype(jnp.int32)
        efield, send = pl.pallas_call(
            yee_kernel,
            out_shape=(
                jax.ShapeDtypeStruct((3, nx, ny, nz), f32),
                jax.ShapeDtypeStruct((sections, CAP * (HIST - HPAST), features), bf16),
            ),
            in_specs=[smem, vmem, smem] + [vmem] * 8,
            out_specs=(vmem, vmem),
            scratch_shapes=[
                pltpu.VMEM((4, planes, tall, nz), f32),
                pltpu.VMEM((3, planes, tall, 2 * nz), f32),
                pltpu.VMEM((3, planes, tall, 2 * nz), f32),
                pltpu.VMEM((planes, tall, 2 * nz), f32),
                pltpu.VMEM((CAP, tiles + 1, CAP * (HIST - HPAST), features), f32),
            ]
            + indices,
            compiler_params=pltpu.CompilerParams(vmem_limit_bytes=24 * MIB),
            name="yee",
        )(place, tile_rows[:, None], owners[:, 0], initial_field, inv_permittivity, xlo, xhi, ylo, yhi, zlo, zhi)

    with jax.named_scope("route_late"):
        late = lax.all_to_all(send, "gx", split_axis=0, concat_axis=0, tiled=True)
        late = late.reshape(sections * CAP * (HIST - HPAST), features)

    with jax.named_scope("project_late"):
        partial = pl.pallas_call(
            project_late,
            grid=(group,),
            out_shape=jax.ShapeDtypeStruct((group, 2 * NB, share // 2), f32),
            in_specs=[
                pl.BlockSpec((sections * 8, features), lambda i: (0, 0)),
                pl.BlockSpec((features, share), lambda i: (0, i)),
                pl.BlockSpec((1, 24, share), lambda i: (i, 0, 0)),
                pl.BlockSpec((slots, 2, group, share // 2), lambda i: (0, 0, 0, 0)),
            ],
            out_specs=pl.BlockSpec((1, 2 * NB, share // 2), lambda i: (i, 0, 0)),
            scratch_shapes=[pltpu.VMEM((3 * 16, features), bf16), pltpu.VMEM((24, share), f32)],
            compiler_params=pltpu.CompilerParams(vmem_limit_bytes=56 * MIB),
            name="project_late",
        )(late, weights, early, lag)

    with jax.named_scope("far"):
        parts = lax.all_to_all(partial, ("gy", "gz"), split_axis=0, concat_axis=0, tiled=True)
        scale = float(tiles * group) ** (-0.5)
        far = pl.pallas_call(
            functools.partial(sum_kernel, scale=scale),
            out_shape=jax.ShapeDtypeStruct((1, NB, share), f32),
            in_specs=[vmem],
            out_specs=vmem,
            compiler_params=pltpu.CompilerParams(vmem_limit_bytes=56 * MIB),
            name="sum",
        )(parts)
    return (efield, far)


def solution(mesh):
    placed = (
        P(None, "gx", "gy", "gz"),
        P("gx", "gy", "gz"),
        P(("gx", "gy", "gz"), None, None),
        P(("gx", "gy", "gz")),
        P(("gx", "gy", "gz"), None),
        P(("gx", "gy", "gz"), None),
        P(),
    )
    return jax.shard_map(
        local,
        mesh=mesh,
        in_specs=placed,
        out_specs=(P(None, "gx", "gy", "gz"), P("gx", None, ("gy", "gz"))),
        check_vma=False,
    )
```

```python
import jax
import jax.numpy as jnp
from jax import lax
from jax.experimental import pallas as pl
from jax.experimental.pallas import tpu as pltpu
from jax.sharding import PartitionSpec as P

STEPS = 4
HIST = 16
HPAST = 12
LAG = 4
NB = 20
CAP = 2
W = 4
COURANT = 0.5
MIB = 1 << 20


def pair(low, high, axis):
    count = lax.axis_size(axis)
    up = [(i, i + 1) for i in range(count - 1)]
    down = [(b, a) for a, b in up]
    return lax.ppermute(high, axis, up), lax.ppermute(low, axis, down)


def assemble(e_ref, eps_ref, xlo_ref, xhi_ref, ylo_ref, yhi_ref, full_ref):
    nx, ny = e_ref.shape[1:3]
    full_ref[:, 0:W, 0:ny, :] = xlo_ref[...]
    full_ref[0:3, W : W + nx, 0:ny, :] = e_ref[...]
    full_ref[3, W : W + nx, 0:ny, :] = eps_ref[...]
    full_ref[:, W + nx :, 0:ny, :] = xhi_ref[...]
    full_ref[:, :, ny : ny + W, :] = yhi_ref[...]
    full_ref[:, :, ny + W :, :] = ylo_ref[...]


def pack_kernel(e_ref, eps_ref, xlo_ref, xhi_ref, ylo_ref, yhi_ref, zlo_ref, zhi_ref, full_ref):
    nx, ny, nz = e_ref.shape[1:]
    planes = nx + 2 * W
    assemble(e_ref, eps_ref, xlo_ref, xhi_ref, ylo_ref, yhi_ref, full_ref)
    groups = nz // W
    lane = lax.broadcasted_iota(jnp.int32, (ny + 2 * W, nz), 1)
    for half in range(4 * planes // groups):
        low = jnp.zeros((ny + 2 * W, nz), jnp.float32)
        high = low
        for g in range(groups):
            at = half * groups + g
            plane = full_ref[at // planes, at % planes]
            mine = (lane >= g * W) & (lane < (g + 1) * W)
            low = jnp.where(mine, pltpu.roll(plane, g * W, 1) if g else plane, low)
            high = jnp.where(mine, pltpu.roll(plane, (g + 1) * W, 1) if g + 1 < groups else plane, high)
        zlo_ref[half] = low
        zhi_ref[half] = high


def slot_sources(owners_ref, src, used):
    tiles = owners_ref.shape[0]

    def clear_src(i, _):
        src[i] = tiles
        return 0

    def clear_used(i, _):
        used[i] = 0
        return 0

    def assign(k, _):
        owner = owners_ref[k]
        rank = used[owner]
        used[owner] = rank + 1
        src[owner * CAP + rank] = k
        return 0

    lax.fori_loop(0, src.shape[0], clear_src, 0)
    lax.fori_loop(0, used.shape[0], clear_used, 0)
    lax.fori_loop(0, tiles, assign, 0)


def early_kernel(owners_ref, past_ref, delays_ref, send_ref, src, used):
    slot_sources(owners_ref, src, used)
    for s in range(send_ref.shape[0]):
        first, second = src[CAP * s], src[CAP * s + 1]
        send_ref[s, 0:32] = past_ref[0, first] + past_ref[1, second]
        send_ref[s, 32:48] = delays_ref[first]
        send_ref[s, 48:64] = delays_ref[second]


def yee_kernel(
    place_ref, rows_ref, owners_ref, e_ref, eps_ref, xlo_ref, xhi_ref, ylo_ref, yhi_ref, zlo_ref, zhi_ref,
    out_ref, send_ref, full, e, h, eps, rec, src, used,
):
    assemble(e_ref, eps_ref, xlo_ref, xhi_ref, ylo_ref, yhi_ref, full)
    nx, ny, nz = out_ref.shape[1:]
    planes = nx + 2 * W
    tall = ny + 2 * W
    wide = 2 * nz
    tiles = rows_ref.shape[0]
    groups = nz // W
    lane = lax.broadcasted_iota(jnp.int32, (tall, nz), 1)
    for at in range(4 * planes):
        c, p, half, g = at // planes, at % planes, at // groups, at % groups
        up = zhi_ref[half]
        down = zlo_ref[half]
        up = pltpu.roll(up, nz - g * W, 1) if g else up
        down = pltpu.roll(down, nz - (g + 1) * W, 1) if g + 1 < groups else down
        beyond = jnp.where(lane < nz // 2, up, down)
        if c < 3:
            e[c, p, :, 0:nz] = full[c, p]
            e[c, p, :, nz:] = beyond
        else:
            eps[p, :, 0:nz] = COURANT * full[c, p]
            eps[p, :, nz:] = COURANT * beyond
    row = lax.broadcasted_iota(jnp.int32, (tall, wide), 0)
    col = lax.broadcasted_iota(jnp.int32, (tall, wide), 1)
    outside = ((row >= ny + W) & (place_ref[1] == 0)) | ((col >= wide - W) & (place_ref[2] == 0))
    mask = jnp.where(outside, 0.0, COURANT)

    def yp(a):
        return pltpu.roll(a, tall - 1, 0)

    def ym(a):
        return pltpu.roll(a, 1, 0)

    def zp(a):
        return pltpu.roll(a, wide - 1, 1)

    def zm(a):
        return pltpu.roll(a, 1, 1)

    rec[...] = jnp.zeros(rec.shape, jnp.float32)
    cell = lax.broadcasted_iota(jnp.int32, (tiles, nx * ny), 1)
    pick = (cell == rows_ref[...]).astype(jnp.bfloat16)
    for step in range(STEPS):

        def magnetic(p, _, step=step):
            ex, ey, ez = e[0, p], e[1, p], e[2, p]
            ey1, ez1 = e[1, p + 1], e[2, p + 1]
            cx = mask * ((yp(ez) - ez) - (zp(ey) - ey))
            cy = mask * ((zp(ex) - ex) - (ez1 - ez))
            cz = mask * ((ey1 - ey) - (yp(ex) - ex))
            if step == 0:
                h[0, p], h[1, p], h[2, p] = -cx, -cy, -cz
            else:
                h[0, p], h[1, p], h[2, p] = h[0, p] - cx, h[1, p] - cy, h[2, p] - cz
            return 0

        def electric(p, _):
            hx, hy, hz = h[0, p], h[1, p], h[2, p]
            hy0, hz0 = h[1, p - 1], h[2, p - 1]
            k = eps[p]
            e[0, p] = e[0, p] + k * ((hz - ym(hz)) - (hy - zm(hy)))
            e[1, p] = e[1, p] + k * ((hx - zm(hx)) - (hz - hz0))
            e[2, p] = e[2, p] + k * ((hy - hy0) - (hx - ym(hx)))
            return 0

        lax.fori_loop(step, planes - 1 - step, magnetic, 0, unroll=4)

        @pl.when(place_ref[0] == 0)
        def _():
            h[:, W - 1] = jnp.zeros((3, tall, wide), jnp.float32)


        parts = [h[c, W : W + nx, 0:ny, 0:nz].reshape(nx * ny, nz) for c in range(2)]
        inner = jnp.concatenate(parts, axis=1).astype(jnp.bfloat16)
        sample = jnp.dot(pick, inner, preferred_element_type=jnp.float32)
        for k in range(tiles):
            for half in range(CAP):
                at = half * (HIST - HPAST) + step
                rec[half, k, at : at + 1, :] = sample[k : k + 1]
        lax.fori_loop(step + 1, planes - 1 - step, electric, 0, unroll=4)
    out_ref[...] = e[:, W : W + nx, 0:ny, 0:nz]

    slot_sources(owners_ref, src, used)
    for s in range(send_ref.shape[0]):
        both = rec[0, src[CAP * s]] + rec[1, src[CAP * s + 1]]
        send_ref[s] = both.astype(jnp.bfloat16)


def delays_of(lag, slot, part):
    rows = [jnp.broadcast_to(lag[slot, i, pl.ds(part, 1), :], (8, lag.shape[3])) for i in range(2)]
    return jnp.concatenate(rows, axis=1)


def add_delayed(sums, values, delay):
    for j in range(1, LAG):
        sums[j - 1] = sums[j - 1] + jnp.where(delay == float(j), values, 0.0)


def split3(total, pieces_ref):
    rows = total.shape[0]
    for i in range(3):
        piece = total.astype(jnp.bfloat16)
        pieces_ref[rows * i : rows * (i + 1)] = piece
        total = total - piece.astype(jnp.float32)


def project_total(pieces_ref, weights):
    parts = jnp.dot(pieces_ref[...], weights, preferred_element_type=jnp.float32)
    rows = parts.shape[0] // 3
    return parts[0:rows] + parts[rows : 2 * rows] + parts[2 * rows :]


def project_early(got_ref, weights_ref, out_ref, lag_ref, pieces):
    pairs, _, features = got_ref.shape
    share = weights_ref.shape[1]
    part = pl.program_id(0)

    @pl.when(part == 0)
    def _():
        def widen(s, total):
            for i in range(CAP):
                wide = got_ref[s, 32 + 16 * i : 48 + 16 * i].astype(jnp.float32)
                lag_ref[CAP * s + i, 0] = wide[:, 0 : share // 2]
                lag_ref[CAP * s + i, 1] = wide[:, share // 2 :]
            return total + got_ref[s, 0:32].astype(jnp.float32)

        total = lax.fori_loop(0, pairs, widen, jnp.zeros((32, features), jnp.float32), unroll=4)
        split3(total, pieces)

    weights = weights_ref[...]
    total = project_total(pieces, weights)
    upper = lax.broadcasted_iota(jnp.int32, (8, share), 0) < HPAST - 8
    low = [jnp.zeros((8, share), jnp.float32)] * (LAG - 1)
    high = list(low)
    block = min(8, pairs)
    for b in range(0, pairs, block):
        rows = got_ref[b : b + block, 0:32, :].reshape(block * 32, features)
        proj = jnp.dot(rows, weights, preferred_element_type=jnp.float32)
        for s in range(block):
            first = delays_of(lag_ref, CAP * (b + s), part)
            second = delays_of(lag_ref, CAP * (b + s) + 1, part)
            add_delayed(low, proj[32 * s : 32 * s + 8], first)
            add_delayed(low, proj[32 * s + 8 : 32 * s + 16], second)
            add_delayed(high, proj[32 * s + 16 : 32 * s + 24], jnp.where(upper, first, second))
    low.insert(0, total[0:8] + total[8:16] - low[0] - low[1] - low[2])
    high.insert(0, total[16:24] - high[0] - high[1] - high[2])
    out_ref[0] = jnp.zeros(out_ref.shape[1:], jnp.float32)
    for j in range(LAG):
        out_ref[0, j : j + 8, :] += low[j]
        out_ref[0, j + 8 : j + HPAST, :] += high[j][0:4] + high[j][4:8]


def project_late(got_ref, weights_ref, early_ref, lag_ref, out_ref, pieces):
    pairs = got_ref.shape[0] // 8
    share = weights_ref.shape[1]
    part = pl.program_id(0)

    @pl.when(part == 0)
    def _():
        wide = got_ref[...].astype(jnp.float32)
        total = wide[0:8]
        for s in range(1, pairs):
            total = total + wide[8 * s : 8 * s + 8]
        split3(jnp.concatenate([total, jnp.zeros_like(total)]), pieces)

    weights = weights_ref[...]
    total = project_total(pieces, weights)[0:8]
    proj = jnp.dot(got_ref[...], weights, preferred_element_type=jnp.float32)
    upper = lax.broadcasted_iota(jnp.int32, (8, share), 0) < HIST - HPAST
    sums = [jnp.zeros((8, share), jnp.float32)] * (LAG - 1)
    for s in range(pairs):
        delay = jnp.where(upper, delays_of(lag_ref, CAP * s, part), delays_of(lag_ref, CAP * s + 1, part))
        add_delayed(sums, proj[8 * s : 8 * s + 8], delay)
    sums.insert(0, total - sums[0] - sums[1] - sums[2])
    out_ref[...] = early_ref[...]
    for j in range(LAG):
        out_ref[0, HPAST + j : HIST + j, :] += sums[j][0:4] + sums[j][4:8]


def local(initial_field, inv_permittivity, history, tile_rows, owners, delays, weights):
    nx, ny, nz = inv_permittivity.shape
    planes, tall = nx + 2 * W, ny + 2 * W
    tiles = history.shape[0]
    sections = lax.axis_size("gx")
    slots = sections * CAP
    group = lax.axis_size(("gy", "gz"))
    features = history.shape[2]
    share = weights.shape[1] // group
    f32, bf16 = jnp.float32, jnp.bfloat16

    smem = pl.BlockSpec(memory_space=pltpu.SMEM)
    vmem = pl.BlockSpec(memory_space=pltpu.VMEM)
    indices = [pltpu.SMEM((slots,), jnp.int32), pltpu.SMEM((sections,), jnp.int32)]
    with jax.named_scope("halo"):
        own = inv_permittivity[None]
        xlo, xhi = pair(
            jnp.concatenate([initial_field[:, :W], own[:, :W]]),
            jnp.concatenate([initial_field[:, nx - W :], own[:, nx - W :]]),
            "gx",
        )

        def rows_of(part):
            mid = jnp.concatenate([initial_field[:, :, part], own[:, :, part]])
            return jnp.concatenate([xlo[:, :, part], mid, xhi[:, :, part]], axis=1)

        ylo, yhi = pair(rows_of(slice(0, W)), rows_of(slice(ny - W, ny)), "gy")
        packs = 4 * planes * W // nz
        zlo, zhi = pl.pallas_call(
            pack_kernel,
            out_shape=(
                jax.ShapeDtypeStruct((packs, tall, nz), f32),
                jax.ShapeDtypeStruct((packs, tall, nz), f32),
            ),
            scratch_shapes=[pltpu.VMEM((4, planes, tall, nz), f32)],
            compiler_params=pltpu.CompilerParams(vmem_limit_bytes=16 * MIB),
            name="pack",
        )(initial_field, inv_permittivity, xlo, xhi, ylo, yhi)
        zlo, zhi = pair(zlo, zhi, "gz")

    with jax.named_scope("route_early"):
        extra = ((0, 1), (0, 0), (0, 0))
        past = jnp.pad(history, extra)

        def gap(rows):
            return jnp.zeros((tiles + 1, rows, features), bf16)

        low, high = past[:, 0:8], past[:, 8:HPAST]
        past = jnp.stack(
            [
                jnp.concatenate([low, gap(8), high, gap(12)], axis=1),
                jnp.concatenate([gap(8), low, gap(4), high, gap(8)], axis=1),
            ]
        )
        lags = jnp.pad(delays.astype(bf16).reshape(tiles, group, share), extra)
        send = pl.pallas_call(
            early_kernel,
            out_shape=jax.ShapeDtypeStruct((sections, 32 + CAP * group, features), bf16),
            in_specs=[smem, vmem, vmem],
            out_specs=vmem,
            scratch_shapes=indices,
            compiler_params=pltpu.CompilerParams(vmem_limit_bytes=8 * MIB),
            name="early",
        )(owners[:, 0], past, lags)
        send, _, _ = lax.optimization_barrier((send, xlo, xhi))
        got = lax.all_to_all(send, "gx", split_axis=0, concat_axis=0, tiled=True)

    with jax.named_scope("project_early"):
        early, lag = pl.pallas_call(
            project_early,
            grid=(group,),
            out_shape=(
                jax.ShapeDtypeStruct((group, 24, share), f32),
                jax.ShapeDtypeStruct((slots, 2, group, share // 2), f32),
            ),
            in_specs=[
                pl.BlockSpec((sections, 32 + CAP * group, features), lambda i: (0, 0, 0)),
                pl.BlockSpec((features, share), lambda i: (0, i)),
            ],
            out_specs=(
                pl.BlockSpec((1, 24, share), lambda i: (i, 0, 0)),
                pl.BlockSpec((slots, 2, group, share // 2), lambda i: (0, 0, 0, 0)),
            ),
            scratch_shapes=[pltpu.VMEM((3 * 32, features), bf16)],
            cost_estimate=pl.CostEstimate(
                flops=2 * slots * HIST * features * share * group, bytes_accessed=30 * MIB, transcendentals=0
            ),
            compiler_params=pltpu.CompilerParams(vmem_limit_bytes=24 * MIB),
            name="project_early",
        )(got, weights)

    with jax.named_scope("steps"):
        place = jnp.stack([lax.axis_index(a) for a in ("gx", "gy", "gz")]).astype(jnp.int32)
        efield, send = pl.pallas_call(
            yee_kernel,
            out_shape=(
                jax.ShapeDtypeStruct((3, nx, ny, nz), f32),
                jax.ShapeDtypeStruct((sections, CAP * (HIST - HPAST), features), bf16),
            ),
            in_specs=[smem, vmem, smem] + [vmem] * 8,
            out_specs=(vmem, vmem),
            scratch_shapes=[
                pltpu.VMEM((4, planes, tall, nz), f32),
                pltpu.VMEM((3, planes, tall, 2 * nz), f32),
                pltpu.VMEM((3, planes, tall, 2 * nz), f32),
                pltpu.VMEM((planes, tall, 2 * nz), f32),
                pltpu.VMEM((CAP, tiles + 1, CAP * (HIST - HPAST), features), f32),
            ]
            + indices,
            compiler_params=pltpu.CompilerParams(vmem_limit_bytes=24 * MIB),
            name="yee",
        )(place, tile_rows[:, None], owners[:, 0], initial_field, inv_permittivity, xlo, xhi, ylo, yhi, zlo, zhi)

    with jax.named_scope("route_late"):
        late = lax.all_to_all(send, "gx", split_axis=0, concat_axis=0, tiled=True)
        late = late.reshape(sections * CAP * (HIST - HPAST), features)

    with jax.named_scope("project_late"):
        partial = pl.pallas_call(
            project_late,
            grid=(group,),
            out_shape=jax.ShapeDtypeStruct((group, 24, share), f32),
            in_specs=[
                pl.BlockSpec((sections * 8, features), lambda i: (0, 0)),
                pl.BlockSpec((features, share), lambda i: (0, i)),
                pl.BlockSpec((1, 24, share), lambda i: (i, 0, 0)),
                pl.BlockSpec((slots, 2, group, share // 2), lambda i: (0, 0, 0, 0)),
            ],
            out_specs=pl.BlockSpec((1, 24, share), lambda i: (i, 0, 0)),
            scratch_shapes=[pltpu.VMEM((3 * 16, features), bf16)],
            input_output_aliases={2: 0},
            compiler_params=pltpu.CompilerParams(vmem_limit_bytes=24 * MIB),
            name="project_late",
        )(late, weights, early, lag)

    with jax.named_scope("far"):
        parts = lax.all_to_all(partial, ("gy", "gz"), split_axis=0, concat_axis=0, tiled=True)
        scale = float(tiles * group) ** (-0.5)
        far = jnp.sum(parts[:, :NB], axis=0) * scale
    return (efield, far[None])


def solution(mesh):
    placed = (
        P(None, "gx", "gy", "gz"),
        P("gx", "gy", "gz"),
        P(("gx", "gy", "gz"), None, None),
        P(("gx", "gy", "gz")),
        P(("gx", "gy", "gz"), None),
        P(("gx", "gy", "gz"), None),
        P(),
    )
    return jax.shard_map(
        local,
        mesh=mesh,
        in_specs=placed,
        out_specs=(P(None, "gx", "gy", "gz"), P("gx", None, ("gy", "gz"))),
        check_vma=False,
    )
```

```python
import jax
import jax.numpy as jnp
from jax import lax
from jax.experimental import pallas as pl
from jax.experimental.pallas import tpu as pltpu
from jax.sharding import PartitionSpec as P

STEPS = 4
HIST = 16
HPAST = 12
LAG = 4
NB = 20
CAP = 2
W = 4
COURANT = 0.5
MIB = 1 << 20


def pair(low, high, axis):
    count = lax.axis_size(axis)
    up = [(i, i + 1) for i in range(count - 1)]
    down = [(b, a) for a, b in up]
    return lax.ppermute(high, axis, up), lax.ppermute(low, axis, down)


def assemble(e_ref, eps_ref, xlo_ref, xhi_ref, ylo_ref, yhi_ref, full_ref):
    nx, ny = e_ref.shape[1:3]
    full_ref[:, 0:W, 0:ny, :] = xlo_ref[...]
    full_ref[0:3, W : W + nx, 0:ny, :] = e_ref[...]
    full_ref[3, W : W + nx, 0:ny, :] = eps_ref[...]
    full_ref[:, W + nx :, 0:ny, :] = xhi_ref[...]
    full_ref[:, :, ny : ny + W, :] = yhi_ref[...]
    full_ref[:, :, ny + W :, :] = ylo_ref[...]


def rows_kernel(e_ref, eps_ref, xlo_ref, xhi_ref, low_ref, high_ref):
    nx, ny = e_ref.shape[1:3]
    for out_ref, rows in ((low_ref, slice(0, W)), (high_ref, slice(ny - W, ny))):
        out_ref[:, 0:W] = xlo_ref[:, :, rows, :]
        out_ref[0:3, W : W + nx] = e_ref[:, :, rows, :]
        out_ref[3, W : W + nx] = eps_ref[:, rows, :]
        out_ref[:, W + nx :] = xhi_ref[:, :, rows, :]


def pack_kernel(e_ref, eps_ref, xlo_ref, xhi_ref, ylo_ref, yhi_ref, zlo_ref, zhi_ref, full_ref):
    nx, ny, nz = e_ref.shape[1:]
    planes = nx + 2 * W
    assemble(e_ref, eps_ref, xlo_ref, xhi_ref, ylo_ref, yhi_ref, full_ref)
    groups = nz // W
    lane = lax.broadcasted_iota(jnp.int32, (ny + 2 * W, nz), 1)
    for half in range(4 * planes // groups):
        low = jnp.zeros((ny + 2 * W, nz), jnp.float32)
        high = low
        for g in range(groups):
            at = half * groups + g
            plane = full_ref[at // planes, at % planes]
            mine = (lane >= g * W) & (lane < (g + 1) * W)
            low = jnp.where(mine, pltpu.roll(plane, g * W, 1) if g else plane, low)
            high = jnp.where(mine, pltpu.roll(plane, (g + 1) * W, 1) if g + 1 < groups else plane, high)
        zlo_ref[half] = low
        zhi_ref[half] = high


def slot_sources(owners_ref, src, used):
    tiles = owners_ref.shape[0]

    def clear_src(i, _):
        src[i] = tiles
        return 0

    def clear_used(i, _):
        used[i] = 0
        return 0

    def assign(k, _):
        owner = owners_ref[k]
        rank = used[owner]
        used[owner] = rank + 1
        src[owner * CAP + rank] = k
        return 0

    lax.fori_loop(0, src.shape[0], clear_src, 0)
    lax.fori_loop(0, used.shape[0], clear_used, 0)
    lax.fori_loop(0, tiles, assign, 0)


def early_kernel(owners_ref, past_ref, delays_ref, send_ref, src, used):
    slot_sources(owners_ref, src, used)
    for s in range(send_ref.shape[0]):
        first, second = src[CAP * s], src[CAP * s + 1]
        send_ref[s, 0:32] = past_ref[0, first] + past_ref[1, second]
        send_ref[s, 32:48] = delays_ref[first]
        send_ref[s, 48:64] = delays_ref[second]


def yee_kernel(
    place_ref, rows_ref, owners_ref, e_ref, eps_ref, xlo_ref, xhi_ref, ylo_ref, yhi_ref, zlo_ref, zhi_ref,
    out_ref, send_ref, full, e, h, eps, rec, src, used,
):
    assemble(e_ref, eps_ref, xlo_ref, xhi_ref, ylo_ref, yhi_ref, full)
    nx, ny, nz = out_ref.shape[1:]
    planes = nx + 2 * W
    tall = ny + 2 * W
    wide = 2 * nz
    tiles = rows_ref.shape[0]
    groups = nz // W
    lane = lax.broadcasted_iota(jnp.int32, (tall, nz), 1)
    for at in range(4 * planes):
        c, p, half, g = at // planes, at % planes, at // groups, at % groups
        up = zhi_ref[half]
        down = zlo_ref[half]
        up = pltpu.roll(up, nz - g * W, 1) if g else up
        down = pltpu.roll(down, nz - (g + 1) * W, 1) if g + 1 < groups else down
        beyond = jnp.where(lane < nz // 2, up, down)
        if c < 3:
            e[c, p, :, 0:nz] = full[c, p]
            e[c, p, :, nz:] = beyond
        else:
            eps[p, :, 0:nz] = COURANT * full[c, p]
            eps[p, :, nz:] = COURANT * beyond
    row = lax.broadcasted_iota(jnp.int32, (tall, wide), 0)
    col = lax.broadcasted_iota(jnp.int32, (tall, wide), 1)
    outside = ((row >= ny + W) & (place_ref[1] == 0)) | ((col >= wide - W) & (place_ref[2] == 0))
    mask = jnp.where(outside, 0.0, COURANT)

    def yp(a):
        return pltpu.roll(a, tall - 1, 0)

    def ym(a):
        return pltpu.roll(a, 1, 0)

    def zp(a):
        return pltpu.roll(a, wide - 1, 1)

    def zm(a):
        return pltpu.roll(a, 1, 1)

    rec[...] = jnp.zeros(rec.shape, jnp.float32)
    cell = lax.broadcasted_iota(jnp.int32, (tiles, nx * ny), 1)
    pick = (cell == rows_ref[...]).astype(jnp.bfloat16)
    for step in range(STEPS):

        def magnetic(p, _, step=step):
            ex, ey, ez = e[0, p], e[1, p], e[2, p]
            ey1, ez1 = e[1, p + 1], e[2, p + 1]
            cx = mask * ((yp(ez) - ez) - (zp(ey) - ey))
            cy = mask * ((zp(ex) - ex) - (ez1 - ez))
            cz = mask * ((ey1 - ey) - (yp(ex) - ex))
            if step == 0:
                h[0, p], h[1, p], h[2, p] = -cx, -cy, -cz
            else:
                h[0, p], h[1, p], h[2, p] = h[0, p] - cx, h[1, p] - cy, h[2, p] - cz
            return 0

        def electric(p, _):
            hx, hy, hz = h[0, p], h[1, p], h[2, p]
            hy0, hz0 = h[1, p - 1], h[2, p - 1]
            k = eps[p]
            e[0, p] = e[0, p] + k * ((hz - ym(hz)) - (hy - zm(hy)))
            e[1, p] = e[1, p] + k * ((hx - zm(hx)) - (hz - hz0))
            e[2, p] = e[2, p] + k * ((hy - hy0) - (hx - ym(hx)))
            return 0

        lax.fori_loop(step, planes - 1 - step, magnetic, 0, unroll=4)

        @pl.when(place_ref[0] == 0)
        def _():
            h[:, W - 1] = jnp.zeros((3, tall, wide), jnp.float32)


        parts = [h[c, W : W + nx, 0:ny, 0:nz].reshape(nx * ny, nz) for c in range(2)]
        inner = jnp.concatenate(parts, axis=1).astype(jnp.bfloat16)
        sample = jnp.dot(pick, inner, preferred_element_type=jnp.float32)
        for k in range(tiles):
            for half in range(CAP):
                at = half * (HIST - HPAST) + step
                rec[half, k, at : at + 1, :] = sample[k : k + 1]
        lax.fori_loop(step + 1, planes - 1 - step, electric, 0, unroll=4)
    out_ref[...] = e[:, W : W + nx, 0:ny, 0:nz]

    slot_sources(owners_ref, src, used)
    for s in range(send_ref.shape[0]):
        both = rec[0, src[CAP * s]] + rec[1, src[CAP * s + 1]]
        send_ref[s] = both.astype(jnp.bfloat16)


def delays_of(lag, slot, part):
    rows = [jnp.broadcast_to(lag[slot, i, pl.ds(part, 1), :], (8, lag.shape[3])) for i in range(2)]
    return jnp.concatenate(rows, axis=1)


def add_delayed(sums, values, delay):
    sums[0] = sums[0] + values
    for j in range(1, LAG):
        sums[j] = sums[j] + jnp.where(delay == float(j), values, 0.0)


def by_delay(sums):
    return [sums[0] - sums[1] - sums[2] - sums[3]] + sums[1:]


def project_early(got_ref, weights_ref, out_ref, lag_ref):
    pairs, _, features = got_ref.shape
    parts = out_ref.shape[0]
    share = weights_ref.shape[1] // parts
    step = pl.program_id(0)

    @pl.when(step == 0)
    def _():
        def widen(s, _):
            for i in range(CAP):
                wide = got_ref[s, 32 + 16 * i : 48 + 16 * i].astype(jnp.float32)
                lag_ref[CAP * s + i, 0] = wide[:, 0 : share // 2]
                lag_ref[CAP * s + i, 1] = wide[:, share // 2 :]
            return 0

        lax.fori_loop(0, pairs, widen, 0, unroll=min(4, pairs))

    upper = lax.broadcasted_iota(jnp.int32, (8, share), 0) < HPAST - 8
    block = min(8, pairs)
    for c in range(parts):
        part = step * parts + c
        weights = weights_ref[:, share * c : share * (c + 1)]
        low = [jnp.zeros((8, share), jnp.float32)] * LAG
        high = list(low)
        for b in range(0, pairs, block):
            rows = got_ref[b : b + block, 0:32, :].reshape(block * 32, features)
            proj = jnp.dot(rows, weights, preferred_element_type=jnp.float32)
            for s in range(block):
                first = delays_of(lag_ref, CAP * (b + s), part)
                second = delays_of(lag_ref, CAP * (b + s) + 1, part)
                add_delayed(low, proj[32 * s : 32 * s + 8], first)
                add_delayed(low, proj[32 * s + 8 : 32 * s + 16], second)
                add_delayed(high, proj[32 * s + 16 : 32 * s + 24], jnp.where(upper, first, second))
        out_ref[c] = jnp.zeros(out_ref.shape[1:], jnp.float32)
        for j, (a, b) in enumerate(zip(by_delay(low), by_delay(high), strict=True)):
            out_ref[c, j : j + 8, :] += a
            out_ref[c, j + 8 : j + HPAST, :] += b[0:4] + b[4:8]


def project_late(got_ref, weights_ref, early_ref, lag_ref, out_ref):
    pairs = got_ref.shape[0] // 8
    parts = out_ref.shape[0]
    share = weights_ref.shape[1] // parts
    step = pl.program_id(0)
    upper = lax.broadcasted_iota(jnp.int32, (8, share), 0) < HIST - HPAST
    for c in range(parts):
        part = step * parts + c
        weights = weights_ref[:, share * c : share * (c + 1)]
        proj = jnp.dot(got_ref[...], weights, preferred_element_type=jnp.float32)
        sums = [jnp.zeros((8, share), jnp.float32)] * LAG
        for s in range(pairs):
            delay = jnp.where(upper, delays_of(lag_ref, CAP * s, part), delays_of(lag_ref, CAP * s + 1, part))
            add_delayed(sums, proj[8 * s : 8 * s + 8], delay)
        out_ref[c] = early_ref[c]
        for j, a in enumerate(by_delay(sums)):
            out_ref[c, HPAST + j : HIST + j, :] += a[0:4] + a[4:8]


def local(initial_field, inv_permittivity, history, tile_rows, owners, delays, weights):
    nx, ny, nz = inv_permittivity.shape
    planes, tall = nx + 2 * W, ny + 2 * W
    tiles = history.shape[0]
    sections = lax.axis_size("gx")
    slots = sections * CAP
    group = lax.axis_size(("gy", "gz"))
    features = history.shape[2]
    share = weights.shape[1] // group
    parts = min(4, group)
    f32, bf16 = jnp.float32, jnp.bfloat16

    smem = pl.BlockSpec(memory_space=pltpu.SMEM)
    vmem = pl.BlockSpec(memory_space=pltpu.VMEM)
    indices = [pltpu.SMEM((slots,), jnp.int32), pltpu.SMEM((sections,), jnp.int32)]
    with jax.named_scope("halo"):
        own = inv_permittivity[None]
        xlo, xhi = pair(
            jnp.concatenate([initial_field[:, :W], own[:, :W]]),
            jnp.concatenate([initial_field[:, nx - W :], own[:, nx - W :]]),
            "gx",
        )

        rows = jax.ShapeDtypeStruct((4, planes, W, nz), f32)
        ylo, yhi = pl.pallas_call(
            rows_kernel,
            out_shape=(rows, rows),
            compiler_params=pltpu.CompilerParams(vmem_limit_bytes=8 * MIB),
            name="rows",
        )(initial_field, inv_permittivity, xlo, xhi)
        ylo, yhi = pair(ylo, yhi, "gy")
        packs = 4 * planes * W // nz
        zlo, zhi = pl.pallas_call(
            pack_kernel,
            out_shape=(
                jax.ShapeDtypeStruct((packs, tall, nz), f32),
                jax.ShapeDtypeStruct((packs, tall, nz), f32),
            ),
            scratch_shapes=[pltpu.VMEM((4, planes, tall, nz), f32)],
            compiler_params=pltpu.CompilerParams(vmem_limit_bytes=16 * MIB),
            name="pack",
        )(initial_field, inv_permittivity, xlo, xhi, ylo, yhi)
        zlo, zhi = pair(zlo, zhi, "gz")

    with jax.named_scope("route_early"):
        extra = ((0, 1), (0, 0), (0, 0))
        past = jnp.pad(history, extra)

        def gap(rows):
            return jnp.zeros((tiles + 1, rows, features), bf16)

        low, high = past[:, 0:8], past[:, 8:HPAST]
        past = jnp.stack(
            [
                jnp.concatenate([low, gap(8), high, gap(12)], axis=1),
                jnp.concatenate([gap(8), low, gap(4), high, gap(8)], axis=1),
            ]
        )
        lags = jnp.pad(delays.astype(bf16).reshape(tiles, group, share), extra)
        send = pl.pallas_call(
            early_kernel,
            out_shape=jax.ShapeDtypeStruct((sections, 32 + CAP * group, features), bf16),
            in_specs=[smem, vmem, vmem],
            out_specs=vmem,
            scratch_shapes=indices,
            compiler_params=pltpu.CompilerParams(vmem_limit_bytes=8 * MIB),
            name="early",
        )(owners[:, 0], past, lags)
        send, _, _ = lax.optimization_barrier((send, xlo, xhi))
        got = lax.all_to_all(send, "gx", split_axis=0, concat_axis=0, tiled=True)

    with jax.named_scope("project_early"):
        early, lag = pl.pallas_call(
            project_early,
            grid=(group // parts,),
            out_shape=(
                jax.ShapeDtypeStruct((group, 24, share), f32),
                jax.ShapeDtypeStruct((slots, 2, group, share // 2), f32),
            ),
            in_specs=[
                pl.BlockSpec((sections, 32 + CAP * group, features), lambda i: (0, 0, 0)),
                pl.BlockSpec((features, parts * share), lambda i: (0, i)),
            ],
            out_specs=(
                pl.BlockSpec((parts, 24, share), lambda i: (i, 0, 0)),
                pl.BlockSpec((slots, 2, group, share // 2), lambda i: (0, 0, 0, 0)),
            ),
            cost_estimate=pl.CostEstimate(
                flops=2 * slots * HIST * features * share * group, bytes_accessed=30 * MIB, transcendentals=0
            ),
            compiler_params=pltpu.CompilerParams(vmem_limit_bytes=24 * MIB),
            name="project_early",
        )(got, weights)

    with jax.named_scope("steps"):
        place = jnp.stack([lax.axis_index(a) for a in ("gx", "gy", "gz")]).astype(jnp.int32)
        efield, send = pl.pallas_call(
            yee_kernel,
            out_shape=(
                jax.ShapeDtypeStruct((3, nx, ny, nz), f32),
                jax.ShapeDtypeStruct((sections, CAP * (HIST - HPAST), features), bf16),
            ),
            in_specs=[smem, vmem, smem] + [vmem] * 8,
            out_specs=(vmem, vmem),
            scratch_shapes=[
                pltpu.VMEM((4, planes, tall, nz), f32),
                pltpu.VMEM((3, planes, tall, 2 * nz), f32),
                pltpu.VMEM((3, planes, tall, 2 * nz), f32),
                pltpu.VMEM((planes, tall, 2 * nz), f32),
                pltpu.VMEM((CAP, tiles + 1, CAP * (HIST - HPAST), features), f32),
            ]
            + indices,
            compiler_params=pltpu.CompilerParams(vmem_limit_bytes=24 * MIB),
            name="yee",
        )(place, tile_rows[:, None], owners[:, 0], initial_field, inv_permittivity, xlo, xhi, ylo, yhi, zlo, zhi)

    with jax.named_scope("route_late"):
        late = lax.all_to_all(send, "gx", split_axis=0, concat_axis=0, tiled=True)
        late = late.reshape(sections * CAP * (HIST - HPAST), features)

    with jax.named_scope("project_late"):
        partial = pl.pallas_call(
            project_late,
            grid=(group // parts,),
            out_shape=jax.ShapeDtypeStruct((group, 24, share), f32),
            in_specs=[
                pl.BlockSpec((sections * 8, features), lambda i: (0, 0)),
                pl.BlockSpec((features, parts * share), lambda i: (0, i)),
                pl.BlockSpec((parts, 24, share), lambda i: (i, 0, 0)),
                pl.BlockSpec((slots, 2, group, share // 2), lambda i: (0, 0, 0, 0)),
            ],
            out_specs=pl.BlockSpec((parts, 24, share), lambda i: (i, 0, 0)),
            input_output_aliases={2: 0},
            compiler_params=pltpu.CompilerParams(vmem_limit_bytes=24 * MIB),
            name="project_late",
        )(late, weights, early, lag)

    with jax.named_scope("far"):
        parts = lax.all_to_all(partial, ("gy", "gz"), split_axis=0, concat_axis=0, tiled=True)
        scale = float(tiles * group) ** (-0.5)
        far = jnp.sum(parts[:, :NB], axis=0) * scale
    return (efield, far[None])


def solution(mesh):
    placed = (
        P(None, "gx", "gy", "gz"),
        P("gx", "gy", "gz"),
        P(("gx", "gy", "gz"), None, None),
        P(("gx", "gy", "gz")),
        P(("gx", "gy", "gz"), None),
        P(("gx", "gy", "gz"), None),
        P(),
    )
    return jax.shard_map(
        local,
        mesh=mesh,
        in_specs=placed,
        out_specs=(P(None, "gx", "gy", "gz"), P("gx", None, ("gy", "gz"))),
        check_vma=False,
    )
```

```python
import functools

import jax
import jax.numpy as jnp
from jax import lax
from jax.experimental import pallas as pl
from jax.experimental.pallas import tpu as pltpu
from jax.sharding import PartitionSpec as P

STEPS = 4
HIST = 16
HPAST = 12
LAG = 4
NB = 20
CAP = 2
W = 4
COURANT = 0.5
MIB = 1 << 20


def pair(low, high, axis):
    count = lax.axis_size(axis)
    up = [(i, i + 1) for i in range(count - 1)]
    down = [(b, a) for a, b in up]
    return lax.ppermute(high, axis, up), lax.ppermute(low, axis, down)


def assemble(e_ref, eps_ref, xlo_ref, xhi_ref, ylo_ref, yhi_ref, full_ref):
    nx, ny = e_ref.shape[1:3]
    full_ref[:, 0:W, 0:ny, :] = xlo_ref[...]
    full_ref[0:3, W : W + nx, 0:ny, :] = e_ref[...]
    full_ref[3, W : W + nx, 0:ny, :] = eps_ref[...]
    full_ref[:, W + nx :, 0:ny, :] = xhi_ref[...]
    full_ref[:, :, ny : ny + W, :] = yhi_ref[...]
    full_ref[:, :, ny + W :, :] = ylo_ref[...]


def rows_kernel(e_ref, eps_ref, xlo_ref, xhi_ref, low_ref, high_ref):
    nx, ny = e_ref.shape[1:3]
    for out_ref, rows in ((low_ref, slice(0, W)), (high_ref, slice(ny - W, ny))):
        out_ref[:, 0:W] = xlo_ref[:, :, rows, :]
        out_ref[0:3, W : W + nx] = e_ref[:, :, rows, :]
        out_ref[3, W : W + nx] = eps_ref[:, rows, :]
        out_ref[:, W + nx :] = xhi_ref[:, :, rows, :]


def pack_kernel(e_ref, eps_ref, xlo_ref, xhi_ref, ylo_ref, yhi_ref, zlo_ref, zhi_ref, full_ref):
    nx, ny, nz = e_ref.shape[1:]
    planes = nx + 2 * W
    assemble(e_ref, eps_ref, xlo_ref, xhi_ref, ylo_ref, yhi_ref, full_ref)
    groups = nz // W
    lane = lax.broadcasted_iota(jnp.int32, (ny + 2 * W, nz), 1)
    for half in range(4 * planes // groups):
        low = jnp.zeros((ny + 2 * W, nz), jnp.float32)
        high = low
        for g in range(groups):
            at = half * groups + g
            plane = full_ref[at // planes, at % planes]
            mine = (lane >= g * W) & (lane < (g + 1) * W)
            low = jnp.where(mine, pltpu.roll(plane, g * W, 1) if g else plane, low)
            high = jnp.where(mine, pltpu.roll(plane, (g + 1) * W, 1) if g + 1 < groups else plane, high)
        zlo_ref[half] = low
        zhi_ref[half] = high


def slot_sources(owners_ref, src, used):
    tiles = owners_ref.shape[0]

    def clear_src(i, _):
        src[i] = tiles
        return 0

    def clear_used(i, _):
        used[i] = 0
        return 0

    def assign(k, _):
        owner = owners_ref[k]
        rank = used[owner]
        used[owner] = rank + 1
        src[owner * CAP + rank] = k
        return 0

    lax.fori_loop(0, src.shape[0], clear_src, 0)
    lax.fori_loop(0, used.shape[0], clear_used, 0)
    lax.fori_loop(0, tiles, assign, 0)


def early_kernel(owners_ref, past_ref, delays_ref, send_ref, src, used):
    slot_sources(owners_ref, src, used)
    for s in range(send_ref.shape[0]):
        first, second = src[CAP * s], src[CAP * s + 1]
        send_ref[s, 0:32] = past_ref[0, first] + past_ref[1, second]
        send_ref[s, 32:48] = delays_ref[first]
        send_ref[s, 48:64] = delays_ref[second]


def yee_kernel(
    place_ref, rows_ref, owners_ref, e_ref, eps_ref, xlo_ref, xhi_ref, ylo_ref, yhi_ref, zlo_ref, zhi_ref,
    out_ref, send_ref, full, e, h, eps, rec, src, used,
):
    assemble(e_ref, eps_ref, xlo_ref, xhi_ref, ylo_ref, yhi_ref, full)
    nx, ny, nz = out_ref.shape[1:]
    planes = nx + 2 * W
    tall = ny + 2 * W
    wide = 2 * nz
    tiles = rows_ref.shape[0]
    groups = nz // W
    lane = lax.broadcasted_iota(jnp.int32, (tall, nz), 1)
    for at in range(4 * planes):
        c, p, half, g = at // planes, at % planes, at // groups, at % groups
        up = zhi_ref[half]
        down = zlo_ref[half]
        up = pltpu.roll(up, nz - g * W, 1) if g else up
        down = pltpu.roll(down, nz - (g + 1) * W, 1) if g + 1 < groups else down
        beyond = jnp.where(lane < nz // 2, up, down)
        if c < 3:
            e[c, p, :, 0:nz] = full[c, p]
            e[c, p, :, nz:] = beyond
        else:
            eps[p, :, 0:nz] = COURANT * full[c, p]
            eps[p, :, nz:] = COURANT * beyond
    row = lax.broadcasted_iota(jnp.int32, (tall, wide), 0)
    col = lax.broadcasted_iota(jnp.int32, (tall, wide), 1)
    outside = ((row >= ny + W) & (place_ref[1] == 0)) | ((col >= wide - W) & (place_ref[2] == 0))
    mask = jnp.where(outside, 0.0, COURANT)

    def yp(a):
        return pltpu.roll(a, tall - 1, 0)

    def ym(a):
        return pltpu.roll(a, 1, 0)

    def zp(a):
        return pltpu.roll(a, wide - 1, 1)

    def zm(a):
        return pltpu.roll(a, 1, 1)

    rec[...] = jnp.zeros(rec.shape, jnp.float32)
    cell = lax.broadcasted_iota(jnp.int32, (tiles, nx * ny), 1)
    pick = (cell == rows_ref[...]).astype(jnp.bfloat16)
    for step in range(STEPS):

        def magnetic(p, _, step=step):
            ex, ey, ez = e[0, p], e[1, p], e[2, p]
            ey1, ez1 = e[1, p + 1], e[2, p + 1]
            cx = mask * ((yp(ez) - ez) - (zp(ey) - ey))
            cy = mask * ((zp(ex) - ex) - (ez1 - ez))
            cz = mask * ((ey1 - ey) - (yp(ex) - ex))
            if step == 0:
                h[0, p], h[1, p], h[2, p] = -cx, -cy, -cz
            else:
                h[0, p], h[1, p], h[2, p] = h[0, p] - cx, h[1, p] - cy, h[2, p] - cz
            return 0

        def electric(p, _):
            hx, hy, hz = h[0, p], h[1, p], h[2, p]
            hy0, hz0 = h[1, p - 1], h[2, p - 1]
            k = eps[p]
            e[0, p] = e[0, p] + k * ((hz - ym(hz)) - (hy - zm(hy)))
            e[1, p] = e[1, p] + k * ((hx - zm(hx)) - (hz - hz0))
            e[2, p] = e[2, p] + k * ((hy - hy0) - (hx - ym(hx)))
            return 0

        lax.fori_loop(step, planes - 1 - step, magnetic, 0, unroll=8)

        @pl.when(place_ref[0] == 0)
        def _():
            h[:, W - 1] = jnp.zeros((3, tall, wide), jnp.float32)


        parts = [h[c, W : W + nx, 0:ny, 0:nz].reshape(nx * ny, nz) for c in range(2)]
        inner = jnp.concatenate(parts, axis=1).astype(jnp.bfloat16)
        sample = jnp.dot(pick, inner, preferred_element_type=jnp.float32)
        for k in range(tiles):
            rec[k, step : step + 1, :] = sample[k : k + 1]
        lax.fori_loop(step + 1, planes - 1 - step, electric, 0, unroll=8)
    out_ref[...] = e[:, W : W + nx, 0:ny, 0:nz]

    slot_sources(owners_ref, src, used)
    for s in range(send_ref.shape[0]):
        both = rec[src[CAP * s]] + pltpu.roll(rec[src[CAP * s + 1]], HIST - HPAST, 0)
        send_ref[s] = both.astype(jnp.bfloat16)


def delays_of(lag, slot, part):
    rows = [jnp.broadcast_to(lag[slot, i, pl.ds(part, 1), :], (8, lag.shape[3])) for i in range(2)]
    return jnp.concatenate(rows, axis=1)


def add_delayed(sums, values, delay):
    sums[0] = sums[0] + values
    for j in range(1, LAG):
        sums[j] = sums[j] + jnp.where(delay == float(j), values, 0.0)


def by_delay(sums):
    return [sums[0] - sums[1] - sums[2] - sums[3]] + sums[1:]


def project_early(got_ref, weights_ref, out_ref, lag_ref):
    pairs, _, features = got_ref.shape
    parts = out_ref.shape[0]
    share = weights_ref.shape[1] // parts
    step = pl.program_id(0)

    @pl.when(step == 0)
    def _():
        def widen(s, _):
            for i in range(CAP):
                wide = got_ref[s, 32 + 16 * i : 48 + 16 * i].astype(jnp.float32)
                lag_ref[CAP * s + i, 0] = wide[:, 0 : share // 2]
                lag_ref[CAP * s + i, 1] = wide[:, share // 2 :]
            return 0

        lax.fori_loop(0, pairs, widen, 0, unroll=min(4, pairs))

    upper = lax.broadcasted_iota(jnp.int32, (8, share), 0) < HPAST - 8
    block = min(8, pairs)
    for c in range(parts):
        part = step * parts + c
        weights = weights_ref[:, share * c : share * (c + 1)]
        low = [jnp.zeros((8, share), jnp.float32)] * LAG
        high = list(low)
        for b in range(0, pairs, block):
            rows = got_ref[b : b + block, 0:32, :].reshape(block * 32, features)
            proj = jnp.dot(rows, weights, preferred_element_type=jnp.float32)
            for s in range(block):
                first = delays_of(lag_ref, CAP * (b + s), part)
                second = delays_of(lag_ref, CAP * (b + s) + 1, part)
                add_delayed(low, proj[32 * s : 32 * s + 8], first)
                add_delayed(low, proj[32 * s + 8 : 32 * s + 16], second)
                add_delayed(high, proj[32 * s + 16 : 32 * s + 24], jnp.where(upper, first, second))
        out_ref[c] = jnp.zeros(out_ref.shape[1:], jnp.float32)
        for j, (a, b) in enumerate(zip(by_delay(low), by_delay(high), strict=True)):
            out_ref[c, j : j + 8, :] += a
            out_ref[c, j + 8 : j + HPAST, :] += b[0:4] + b[4:8]


def project_late(got_ref, weights_ref, early_ref, lag_ref, out_ref, *, scale):
    pairs = got_ref.shape[0] // 8
    parts = out_ref.shape[0]
    share = weights_ref.shape[1] // parts
    step = pl.program_id(0)
    upper = lax.broadcasted_iota(jnp.int32, (8, share), 0) < HIST - HPAST
    for c in range(parts):
        part = step * parts + c
        weights = weights_ref[:, share * c : share * (c + 1)]
        proj = jnp.dot(got_ref[...], weights, preferred_element_type=jnp.float32)
        sums = [jnp.zeros((8, share), jnp.float32)] * LAG
        for s in range(pairs):
            delay = jnp.where(upper, delays_of(lag_ref, CAP * s, part), delays_of(lag_ref, CAP * s + 1, part))
            add_delayed(sums, proj[8 * s : 8 * s + 8], delay)
        out_ref[c] = early_ref[c]
        for j, a in enumerate(by_delay(sums)):
            out_ref[c, HPAST + j : HIST + j, :] += a[0:4] + a[4:8]
        out_ref[c] *= scale


def local(initial_field, inv_permittivity, history, tile_rows, owners, delays, weights):
    nx, ny, nz = inv_permittivity.shape
    planes, tall = nx + 2 * W, ny + 2 * W
    tiles = history.shape[0]
    sections = lax.axis_size("gx")
    slots = sections * CAP
    group = lax.axis_size(("gy", "gz"))
    features = history.shape[2]
    share = weights.shape[1] // group
    parts = min(4, group)
    f32, bf16 = jnp.float32, jnp.bfloat16

    smem = pl.BlockSpec(memory_space=pltpu.SMEM)
    vmem = pl.BlockSpec(memory_space=pltpu.VMEM)
    indices = [pltpu.SMEM((slots,), jnp.int32), pltpu.SMEM((sections,), jnp.int32)]
    with jax.named_scope("halo"):
        own = inv_permittivity[None]
        xlo, xhi = pair(
            jnp.concatenate([initial_field[:, :W], own[:, :W]]),
            jnp.concatenate([initial_field[:, nx - W :], own[:, nx - W :]]),
            "gx",
        )

        rows = jax.ShapeDtypeStruct((4, planes, W, nz), f32)
        ylo, yhi = pl.pallas_call(
            rows_kernel,
            out_shape=(rows, rows),
            compiler_params=pltpu.CompilerParams(vmem_limit_bytes=8 * MIB),
            name="rows",
        )(initial_field, inv_permittivity, xlo, xhi)
        ylo, yhi = pair(ylo, yhi, "gy")
        packs = 4 * planes * W // nz
        zlo, zhi = pl.pallas_call(
            pack_kernel,
            out_shape=(
                jax.ShapeDtypeStruct((packs, tall, nz), f32),
                jax.ShapeDtypeStruct((packs, tall, nz), f32),
            ),
            scratch_shapes=[pltpu.VMEM((4, planes, tall, nz), f32)],
            compiler_params=pltpu.CompilerParams(vmem_limit_bytes=16 * MIB),
            name="pack",
        )(initial_field, inv_permittivity, xlo, xhi, ylo, yhi)
        zlo, zhi = pair(zlo, zhi, "gz")

    with jax.named_scope("route_early"):
        extra = ((0, 1), (0, 0), (0, 0))
        past = jnp.pad(history, extra)

        def gap(rows):
            return jnp.zeros((tiles + 1, rows, features), bf16)

        low, high = past[:, 0:8], past[:, 8:HPAST]
        past = jnp.stack(
            [
                jnp.concatenate([low, gap(8), high, gap(12)], axis=1),
                jnp.concatenate([gap(8), low, gap(4), high, gap(8)], axis=1),
            ]
        )
        lags = jnp.pad(delays.astype(bf16).reshape(tiles, group, share), extra)
        send = pl.pallas_call(
            early_kernel,
            out_shape=jax.ShapeDtypeStruct((sections, 32 + CAP * group, features), bf16),
            in_specs=[smem, vmem, vmem],
            out_specs=vmem,
            scratch_shapes=indices,
            compiler_params=pltpu.CompilerParams(vmem_limit_bytes=8 * MIB),
            name="early",
        )(owners[:, 0], past, lags)
        send, _, _ = lax.optimization_barrier((send, xlo, xhi))
        got = lax.all_to_all(send, "gx", split_axis=0, concat_axis=0, tiled=True)

    with jax.named_scope("project_early"):
        early, lag = pl.pallas_call(
            project_early,
            grid=(group // parts,),
            out_shape=(
                jax.ShapeDtypeStruct((group, 24, share), f32),
                jax.ShapeDtypeStruct((slots, 2, group, share // 2), f32),
            ),
            in_specs=[
                pl.BlockSpec((sections, 32 + CAP * group, features), lambda i: (0, 0, 0)),
                pl.BlockSpec((features, parts * share), lambda i: (0, i)),
            ],
            out_specs=(
                pl.BlockSpec((parts, 24, share), lambda i: (i, 0, 0)),
                pl.BlockSpec((slots, 2, group, share // 2), lambda i: (0, 0, 0, 0)),
            ),
            cost_estimate=pl.CostEstimate(
                flops=2 * slots * HIST * features * share * group, bytes_accessed=30 * MIB, transcendentals=0
            ),
            compiler_params=pltpu.CompilerParams(vmem_limit_bytes=24 * MIB),
            name="project_early",
        )(got, weights)

    with jax.named_scope("steps"):
        place = jnp.stack([lax.axis_index(a) for a in ("gx", "gy", "gz")]).astype(jnp.int32)
        efield, send = pl.pallas_call(
            yee_kernel,
            out_shape=(
                jax.ShapeDtypeStruct((3, nx, ny, nz), f32),
                jax.ShapeDtypeStruct((sections, CAP * (HIST - HPAST), features), bf16),
            ),
            in_specs=[smem, vmem, smem] + [vmem] * 8,
            out_specs=(vmem, vmem),
            scratch_shapes=[
                pltpu.VMEM((4, planes, tall, nz), f32),
                pltpu.VMEM((3, planes, tall, 2 * nz), f32),
                pltpu.VMEM((3, planes, tall, 2 * nz), f32),
                pltpu.VMEM((planes, tall, 2 * nz), f32),
                pltpu.VMEM((tiles + 1, CAP * (HIST - HPAST), features), f32),
            ]
            + indices,
            compiler_params=pltpu.CompilerParams(vmem_limit_bytes=24 * MIB),
            name="yee",
        )(place, tile_rows[:, None], owners[:, 0], initial_field, inv_permittivity, xlo, xhi, ylo, yhi, zlo, zhi)

    with jax.named_scope("route_late"):
        late = lax.all_to_all(send, "gx", split_axis=0, concat_axis=0, tiled=True)
        late = late.reshape(sections * CAP * (HIST - HPAST), features)

    with jax.named_scope("project_late"):
        partial = pl.pallas_call(
            functools.partial(project_late, scale=float(tiles * group) ** (-0.5)),
            grid=(group // parts,),
            out_shape=jax.ShapeDtypeStruct((group, 24, share), f32),
            in_specs=[
                pl.BlockSpec((sections * 8, features), lambda i: (0, 0)),
                pl.BlockSpec((features, parts * share), lambda i: (0, i)),
                pl.BlockSpec((parts, 24, share), lambda i: (i, 0, 0)),
                pl.BlockSpec((slots, 2, group, share // 2), lambda i: (0, 0, 0, 0)),
            ],
            out_specs=pl.BlockSpec((parts, 24, share), lambda i: (i, 0, 0)),
            input_output_aliases={2: 0},
            compiler_params=pltpu.CompilerParams(vmem_limit_bytes=24 * MIB),
            name="project_late",
        )(late, weights, early, lag)

    with jax.named_scope("far"):
        parts = lax.all_to_all(partial, ("gy", "gz"), split_axis=0, concat_axis=0, tiled=True)
        far = jnp.sum(parts[:, :NB], axis=0, keepdims=True)
    return (efield, far)


def solution(mesh):
    placed = (
        P(None, "gx", "gy", "gz"),
        P("gx", "gy", "gz"),
        P(("gx", "gy", "gz"), None, None),
        P(("gx", "gy", "gz")),
        P(("gx", "gy", "gz"), None),
        P(("gx", "gy", "gz"), None),
        P(),
    )
    return jax.shard_map(
        local,
        mesh=mesh,
        in_specs=placed,
        out_specs=(P(None, "gx", "gy", "gz"), P("gx", None, ("gy", "gz"))),
        check_vma=False,
    )
```

```python
import functools

import jax
import jax.numpy as jnp
from jax import lax
from jax.experimental import pallas as pl
from jax.experimental.pallas import tpu as pltpu
from jax.sharding import PartitionSpec as P

STEPS = 4
HIST = 16
HPAST = 12
LAG = 4
NB = 20
CAP = 2
W = 4
COURANT = 0.5
MIB = 1 << 20


def pair(low, high, axis):
    count = lax.axis_size(axis)
    up = [(i, i + 1) for i in range(count - 1)]
    down = [(b, a) for a, b in up]
    return lax.ppermute(high, axis, up), lax.ppermute(low, axis, down)


def assemble(e_ref, eps_ref, xlo_ref, xhi_ref, ylo_ref, yhi_ref, full_ref):
    nx, ny = e_ref.shape[1:3]
    full_ref[:, 0:W, 0:ny, :] = xlo_ref[...]
    full_ref[0:3, W : W + nx, 0:ny, :] = e_ref[...]
    full_ref[3, W : W + nx, 0:ny, :] = eps_ref[...]
    full_ref[:, W + nx :, 0:ny, :] = xhi_ref[...]
    full_ref[:, :, ny : ny + W, :] = yhi_ref[...]
    full_ref[:, :, ny + W :, :] = ylo_ref[...]


def rows_kernel(e_ref, eps_ref, xlo_ref, xhi_ref, low_ref, high_ref):
    nx, ny = e_ref.shape[1:3]
    for out_ref, rows in ((low_ref, slice(0, W)), (high_ref, slice(ny - W, ny))):
        out_ref[:, 0:W] = xlo_ref[:, :, rows, :]
        out_ref[0:3, W : W + nx] = e_ref[:, :, rows, :]
        out_ref[3, W : W + nx] = eps_ref[:, rows, :]
        out_ref[:, W + nx :] = xhi_ref[:, :, rows, :]


def pack_kernel(e_ref, eps_ref, xlo_ref, xhi_ref, ylo_ref, yhi_ref, zlo_ref, zhi_ref, full_ref):
    nx, ny, nz = e_ref.shape[1:]
    planes = nx + 2 * W
    assemble(e_ref, eps_ref, xlo_ref, xhi_ref, ylo_ref, yhi_ref, full_ref)
    groups = nz // W
    lane = lax.broadcasted_iota(jnp.int32, (ny + 2 * W, nz), 1)
    for half in range(4 * planes // groups):
        low = jnp.zeros((ny + 2 * W, nz), jnp.float32)
        high = low
        for g in range(groups):
            at = half * groups + g
            plane = full_ref[at // planes, at % planes]
            mine = (lane >= g * W) & (lane < (g + 1) * W)
            low = jnp.where(mine, pltpu.roll(plane, g * W, 1) if g else plane, low)
            high = jnp.where(mine, pltpu.roll(plane, (g + 1) * W, 1) if g + 1 < groups else plane, high)
        zlo_ref[half] = low
        zhi_ref[half] = high


def slot_sources(owners_ref, src, used):
    tiles = owners_ref.shape[0]

    def clear_src(i, _):
        src[i] = tiles
        return 0

    def clear_used(i, _):
        used[i] = 0
        return 0

    def assign(k, _):
        owner = owners_ref[k]
        rank = used[owner]
        used[owner] = rank + 1
        src[owner * CAP + rank] = k
        return 0

    lax.fori_loop(0, src.shape[0], clear_src, 0)
    lax.fori_loop(0, used.shape[0], clear_used, 0)
    lax.fori_loop(0, tiles, assign, 0)


def early_kernel(owners_ref, past_ref, delays_ref, send_ref, src, used):
    slot_sources(owners_ref, src, used)
    for s in range(send_ref.shape[0]):
        first, second = src[CAP * s], src[CAP * s + 1]
        send_ref[s, 0:32] = past_ref[0, first] + past_ref[1, second]
        send_ref[s, 32:48] = delays_ref[first]
        send_ref[s, 48:64] = delays_ref[second]


def yee_kernel(
    place_ref, rows_ref, owners_ref, e_ref, eps_ref, xlo_ref, xhi_ref, ylo_ref, yhi_ref, zlo_ref, zhi_ref,
    out_ref, send_ref, full, e, h, eps, rec, src, used,
):
    assemble(e_ref, eps_ref, xlo_ref, xhi_ref, ylo_ref, yhi_ref, full)
    nx, ny, nz = out_ref.shape[1:]
    planes = nx + 2 * W
    tall = ny + 2 * W
    wide = 2 * nz
    tiles = rows_ref.shape[0]
    groups = nz // W
    lane = lax.broadcasted_iota(jnp.int32, (tall, nz), 1)
    for at in range(4 * planes):
        c, p, half, g = at // planes, at % planes, at // groups, at % groups
        up = zhi_ref[half]
        down = zlo_ref[half]
        up = pltpu.roll(up, nz - g * W, 1) if g else up
        down = pltpu.roll(down, nz - (g + 1) * W, 1) if g + 1 < groups else down
        beyond = jnp.where(lane < nz // 2, up, down)
        if c < 3:
            e[c, p, :, 0:nz] = full[c, p]
            e[c, p, :, nz:] = beyond
        else:
            eps[p, :, 0:nz] = COURANT * full[c, p]
            eps[p, :, nz:] = COURANT * beyond
    row = lax.broadcasted_iota(jnp.int32, (tall, wide), 0)
    col = lax.broadcasted_iota(jnp.int32, (tall, wide), 1)
    outside = ((row >= ny + W) & (place_ref[1] == 0)) | ((col >= wide - W) & (place_ref[2] == 0))
    mask = jnp.where(outside, 0.0, COURANT)

    def yp(a):
        return pltpu.roll(a, tall - 1, 0)

    def ym(a):
        return pltpu.roll(a, 1, 0)

    def zp(a):
        return pltpu.roll(a, wide - 1, 1)

    def zm(a):
        return pltpu.roll(a, 1, 1)

    rec[...] = jnp.zeros(rec.shape, jnp.float32)
    cell = lax.broadcasted_iota(jnp.int32, (tiles, nx * ny), 1)
    pick = (cell == rows_ref[...]).astype(jnp.bfloat16)
    for step in range(STEPS):

        def magnetic(p, _, step=step):
            ex, ey, ez = e[0, p], e[1, p], e[2, p]
            ey1, ez1 = e[1, p + 1], e[2, p + 1]
            cx = mask * ((yp(ez) - ez) - (zp(ey) - ey))
            cy = mask * ((zp(ex) - ex) - (ez1 - ez))
            cz = mask * ((ey1 - ey) - (yp(ex) - ex))
            if step == 0:
                h[0, p], h[1, p], h[2, p] = -cx, -cy, -cz
            else:
                h[0, p], h[1, p], h[2, p] = h[0, p] - cx, h[1, p] - cy, h[2, p] - cz
            return 0

        def electric(p, _):
            hx, hy, hz = h[0, p], h[1, p], h[2, p]
            hy0, hz0 = h[1, p - 1], h[2, p - 1]
            k = eps[p]
            e[0, p] = e[0, p] + k * ((hz - ym(hz)) - (hy - zm(hy)))
            e[1, p] = e[1, p] + k * ((hx - zm(hx)) - (hz - hz0))
            e[2, p] = e[2, p] + k * ((hy - hy0) - (hx - ym(hx)))
            return 0

        lax.fori_loop(step, planes - 1 - step, magnetic, 0, unroll=8)

        @pl.when(place_ref[0] == 0)
        def _():
            h[:, W - 1] = jnp.zeros((3, tall, wide), jnp.float32)


        parts = [h[c, W : W + nx, 0:ny, 0:nz].reshape(nx * ny, nz) for c in range(2)]
        inner = jnp.concatenate(parts, axis=1).astype(jnp.bfloat16)
        sample = jnp.dot(pick, inner, preferred_element_type=jnp.float32)
        for k in range(tiles):
            rec[k, step : step + 1, :] = sample[k : k + 1]
        lax.fori_loop(step + 1, planes - 1 - step, electric, 0, unroll=8)
    out_ref[...] = e[:, W : W + nx, 0:ny, 0:nz]

    slot_sources(owners_ref, src, used)
    for s in range(send_ref.shape[0]):
        both = rec[src[CAP * s]] + pltpu.roll(rec[src[CAP * s + 1]], HIST - HPAST, 0)
        send_ref[s] = both.astype(jnp.bfloat16)


def delays_of(lag, slot, part):
    rows = [jnp.broadcast_to(lag[slot, i, pl.ds(part, 1), :], (8, lag.shape[3])) for i in range(2)]
    return jnp.concatenate(rows, axis=1)


def add_delayed(sums, values, delay):
    sums[0] = sums[0] + values
    for j in range(1, LAG):
        sums[j] = sums[j] + jnp.where(delay == float(j), values, 0.0)


def by_delay(sums):
    return [sums[0] - sums[1] - sums[2] - sums[3]] + sums[1:]


def project_early(got_ref, weights_ref, out_ref, lag_ref):
    pairs, _, features = got_ref.shape
    parts = out_ref.shape[0]
    share = weights_ref.shape[1] // parts
    step = pl.program_id(0)

    @pl.when(step == 0)
    def _():
        def widen(s, _):
            for i in range(CAP):
                wide = got_ref[s, 32 + 16 * i : 48 + 16 * i].astype(jnp.float32)
                lag_ref[CAP * s + i, 0] = wide[:, 0 : share // 2]
                lag_ref[CAP * s + i, 1] = wide[:, share // 2 :]
            return 0

        lax.fori_loop(0, pairs, widen, 0, unroll=min(4, pairs))

    upper = lax.broadcasted_iota(jnp.int32, (8, share), 0) < HPAST - 8
    block = min(8, pairs)
    for c in range(parts):
        part = step * parts + c
        weights = weights_ref[:, share * c : share * (c + 1)]
        low = [jnp.zeros((8, share), jnp.float32)] * LAG
        high = list(low)
        for b in range(0, pairs, block):
            rows = got_ref[b : b + block, 0:32, :].reshape(block * 32, features)
            proj = jnp.dot(rows, weights, preferred_element_type=jnp.float32)
            for s in range(block):
                first = delays_of(lag_ref, CAP * (b + s), part)
                second = delays_of(lag_ref, CAP * (b + s) + 1, part)
                add_delayed(low, proj[32 * s : 32 * s + 8], first)
                add_delayed(low, proj[32 * s + 8 : 32 * s + 16], second)
                add_delayed(high, proj[32 * s + 16 : 32 * s + 24], jnp.where(upper, first, second))
        out_ref[c] = jnp.zeros(out_ref.shape[1:], jnp.float32)
        for j, (a, b) in enumerate(zip(by_delay(low), by_delay(high), strict=True)):
            out_ref[c, j : j + 8, :] += a
            out_ref[c, j + 8 : j + HPAST, :] += b[0:4] + b[4:8]


def project_late(got_ref, weights_ref, early_ref, lag_ref, out_ref, *, scale):
    pairs = got_ref.shape[0] // 8
    parts = out_ref.shape[0]
    share = weights_ref.shape[1] // parts
    step = pl.program_id(0)
    upper = lax.broadcasted_iota(jnp.int32, (8, share), 0) < HIST - HPAST
    for c in range(parts):
        part = step * parts + c
        weights = weights_ref[:, share * c : share * (c + 1)]
        proj = jnp.dot(got_ref[...], weights, preferred_element_type=jnp.float32)
        sums = [jnp.zeros((8, share), jnp.float32)] * LAG
        for s in range(pairs):
            delay = jnp.where(upper, delays_of(lag_ref, CAP * s, part), delays_of(lag_ref, CAP * s + 1, part))
            add_delayed(sums, proj[8 * s : 8 * s + 8], delay)
        out_ref[c] = early_ref[c]
        for j, a in enumerate(by_delay(sums)):
            out_ref[c, HPAST + j : HIST + j, :] += a[0:4] + a[4:8]
        out_ref[c] *= scale


def local(initial_field, inv_permittivity, history, tile_rows, owners, delays, weights):
    nx, ny, nz = inv_permittivity.shape
    planes, tall = nx + 2 * W, ny + 2 * W
    tiles = history.shape[0]
    sections = lax.axis_size("gx")
    slots = sections * CAP
    group = lax.axis_size(("gy", "gz"))
    features = history.shape[2]
    share = weights.shape[1] // group
    parts = min(4, group)
    f32, bf16 = jnp.float32, jnp.bfloat16

    smem = pl.BlockSpec(memory_space=pltpu.SMEM)
    vmem = pl.BlockSpec(memory_space=pltpu.VMEM)
    indices = [pltpu.SMEM((slots,), jnp.int32), pltpu.SMEM((sections,), jnp.int32)]
    with jax.named_scope("halo"):
        own = inv_permittivity[None]
        xlo, xhi = pair(
            jnp.concatenate([initial_field[:, :W], own[:, :W]]),
            jnp.concatenate([initial_field[:, nx - W :], own[:, nx - W :]]),
            "gx",
        )

        rows = jax.ShapeDtypeStruct((4, planes, W, nz), f32)
        ylo, yhi = pl.pallas_call(
            rows_kernel,
            out_shape=(rows, rows),
            compiler_params=pltpu.CompilerParams(vmem_limit_bytes=8 * MIB),
            name="rows",
        )(initial_field, inv_permittivity, xlo, xhi)
        ylo, yhi = pair(ylo, yhi, "gy")
        packs = 4 * planes * W // nz
        zlo, zhi = pl.pallas_call(
            pack_kernel,
            out_shape=(
                jax.ShapeDtypeStruct((packs, tall, nz), f32),
                jax.ShapeDtypeStruct((packs, tall, nz), f32),
            ),
            scratch_shapes=[pltpu.VMEM((4, planes, tall, nz), f32)],
            compiler_params=pltpu.CompilerParams(vmem_limit_bytes=16 * MIB),
            name="pack",
        )(initial_field, inv_permittivity, xlo, xhi, ylo, yhi)
        zlo, zhi = pair(zlo, zhi, "gz")

    with jax.named_scope("route_early"):
        extra = ((0, 1), (0, 0), (0, 0))
        past = jnp.pad(history, extra)

        def gap(rows):
            return jnp.zeros((tiles + 1, rows, features), bf16)

        low, high = past[:, 0:8], past[:, 8:HPAST]
        past = jnp.stack(
            [
                jnp.concatenate([low, gap(8), high, gap(12)], axis=1),
                jnp.concatenate([gap(8), low, gap(4), high, gap(8)], axis=1),
            ]
        )
        lags = jnp.pad(delays.astype(bf16).reshape(tiles, group, share), extra)
        send = pl.pallas_call(
            early_kernel,
            out_shape=jax.ShapeDtypeStruct((sections, 32 + CAP * group, features), bf16),
            in_specs=[smem, vmem, vmem],
            out_specs=vmem,
            scratch_shapes=indices,
            compiler_params=pltpu.CompilerParams(vmem_limit_bytes=8 * MIB),
            name="early",
        )(owners[:, 0], past, lags)
        send, _, _ = lax.optimization_barrier((send, ylo, yhi))
        got = lax.all_to_all(send, "gx", split_axis=0, concat_axis=0, tiled=True)

    with jax.named_scope("project_early"):
        early, lag = pl.pallas_call(
            project_early,
            grid=(group // parts,),
            out_shape=(
                jax.ShapeDtypeStruct((group, 24, share), f32),
                jax.ShapeDtypeStruct((slots, 2, group, share // 2), f32),
            ),
            in_specs=[
                pl.BlockSpec((sections, 32 + CAP * group, features), lambda i: (0, 0, 0)),
                pl.BlockSpec((features, parts * share), lambda i: (0, i)),
            ],
            out_specs=(
                pl.BlockSpec((parts, 24, share), lambda i: (i, 0, 0)),
                pl.BlockSpec((slots, 2, group, share // 2), lambda i: (0, 0, 0, 0)),
            ),
            cost_estimate=pl.CostEstimate(
                flops=2 * slots * HIST * features * share * group, bytes_accessed=30 * MIB, transcendentals=0
            ),
            compiler_params=pltpu.CompilerParams(vmem_limit_bytes=24 * MIB),
            name="project_early",
        )(got, weights)

    with jax.named_scope("steps"):
        place = jnp.stack([lax.axis_index(a) for a in ("gx", "gy", "gz")]).astype(jnp.int32)
        efield, send = pl.pallas_call(
            yee_kernel,
            out_shape=(
                jax.ShapeDtypeStruct((3, nx, ny, nz), f32),
                jax.ShapeDtypeStruct((sections, CAP * (HIST - HPAST), features), bf16),
            ),
            in_specs=[smem, vmem, smem] + [vmem] * 8,
            out_specs=(vmem, vmem),
            scratch_shapes=[
                pltpu.VMEM((4, planes, tall, nz), f32),
                pltpu.VMEM((3, planes, tall, 2 * nz), f32),
                pltpu.VMEM((3, planes, tall, 2 * nz), f32),
                pltpu.VMEM((planes, tall, 2 * nz), f32),
                pltpu.VMEM((tiles + 1, CAP * (HIST - HPAST), features), f32),
            ]
            + indices,
            compiler_params=pltpu.CompilerParams(vmem_limit_bytes=24 * MIB),
            name="yee",
        )(place, tile_rows[:, None], owners[:, 0], initial_field, inv_permittivity, xlo, xhi, ylo, yhi, zlo, zhi)

    with jax.named_scope("route_late"):
        late = lax.all_to_all(send, "gx", split_axis=0, concat_axis=0, tiled=True)
        late = late.reshape(sections * CAP * (HIST - HPAST), features)

    with jax.named_scope("project_late"):
        partial = pl.pallas_call(
            functools.partial(project_late, scale=float(tiles * group) ** (-0.5)),
            grid=(group // parts,),
            out_shape=jax.ShapeDtypeStruct((group, 24, share), f32),
            in_specs=[
                pl.BlockSpec((sections * 8, features), lambda i: (0, 0)),
                pl.BlockSpec((features, parts * share), lambda i: (0, i)),
                pl.BlockSpec((parts, 24, share), lambda i: (i, 0, 0)),
                pl.BlockSpec((slots, 2, group, share // 2), lambda i: (0, 0, 0, 0)),
            ],
            out_specs=pl.BlockSpec((parts, 24, share), lambda i: (i, 0, 0)),
            input_output_aliases={2: 0},
            compiler_params=pltpu.CompilerParams(vmem_limit_bytes=24 * MIB),
            name="project_late",
        )(late, weights, early, lag)

    with jax.named_scope("far"):
        parts = lax.all_to_all(partial, ("gy", "gz"), split_axis=0, concat_axis=0, tiled=True)
        far = jnp.sum(parts[:, :NB], axis=0, keepdims=True)
    return (efield, far)


def solution(mesh):
    placed = (
        P(None, "gx", "gy", "gz"),
        P("gx", "gy", "gz"),
        P(("gx", "gy", "gz"), None, None),
        P(("gx", "gy", "gz")),
        P(("gx", "gy", "gz"), None),
        P(("gx", "gy", "gz"), None),
        P(),
    )
    return jax.shard_map(
        local,
        mesh=mesh,
        in_specs=placed,
        out_specs=(P(None, "gx", "gy", "gz"), P("gx", None, ("gy", "gz"))),
        check_vma=False,
    )
```
